256 devices in a mesh: prompt: 8 (over z_hi, core), resp: 16 (over y, x), grp: 2 (over z_lo).
Axes of the slice: x: 4, y: 4, z: 8 (z_hi: 4, z_lo: 2; z = z_hi * 2 + z_lo), core: 2. Of those that a mesh axis runs over, the one named last changes fastest.
Arguments:
- queries: bfloat16 [32, 1024, 4096], P(('grp', 'resp'), 'prompt'), parts along dimension 0, may hold values from -5 to 5
- response_key_rows: bfloat16 [32, 1024, 512], P(('grp', 'resp'), 'prompt'), parts along dimension 0, may hold values from -6 to 6
- response_value_rows: bfloat16 [32, 1024, 512], P(('grp', 'resp'), 'prompt'), parts along dimension 0, may hold values from -24 to 24
- prompt_keys: bfloat16 [2048, 512], P(('grp', 'prompt', 'resp')), parts along dimension 0, may hold values from -18 to 18
- prompt_value_rows: bfloat16 [2048, 512], P(('grp', 'prompt', 'resp')), parts along dimension 0, may hold values from -24 to 24
- out_grad: bfloat16 [32, 1024, 4096], P(('grp', 'resp'), 'prompt'), parts along dimension 0, may hold values from -6 to 6
- lengths: int32 [32], P('grp'), parts along dimension 0, may hold values from 128 to 1024
Outputs:
- attended: bfloat16 [32, 1024, 4096], P(('grp', 'resp'), 'prompt'), parts along dimension 0
- query_grad: bfloat16 [32, 1024, 4096], P(('grp', 'resp'), 'prompt'), parts along dimension 0
- resp_key_grad: bfloat16 [32, 1024, 512], P(('grp', 'resp'), 'prompt'), parts along dimension 0
- resp_value_grad: bfloat16 [32, 1024, 512], P(('grp', 'resp'), 'prompt'), parts along dimension 0
- prompt_key_grad: float32 [2048, 512], P(('grp', 'prompt', 'resp')), parts along dimension 0
- prompt_value_grad: float32 [2048, 512], P(('grp', 'prompt', 'resp')), parts along dimension 0
The draws below stay inside these ranges and needn't reach their ends.
There are 2 independent parts, one for each index of `grp`. The reference program is written for one: setup_inputs(seed, part) draws one part's arguments, and reference() takes and returns one part's arrays. A program takes and returns all parts, laid end to end along the dimension named above; each array names one. Nothing has to cross between parts.
All inputs are finite; a program needn't handle non-finite values.
Results may differ from the reference program's by a relative error of at most 0.02.
The reference program's roundings to bfloat16 on the way count: a program that leaves them out, or rounds other values in their place, can miss the bound.
Values may be sent and summed in bfloat16 or wider, within the bound.
A program may use at most 128 MiB of HBM per device.

```python
import jax
import jax.numpy as jnp
from jax import lax

QUERY_HEAD_COUNT = 32
SHARED_KV_HEADS = 4
HEAD_SIZE = 128
RT = 128
PROMPT_TOKENS = 1024
RESPONSE_LENGTH = 1024
RESPONSE_COUNT = 16


def draw_queries(key, part):
    key = jax.random.fold_in(key, 11)
    drawn_sample = jnp.clip(jax.random.normal(key, (RESPONSE_COUNT, RESPONSE_LENGTH, QUERY_HEAD_COUNT, HEAD_SIZE), jnp.float32), -5.0, 5.0)
    return drawn_sample.reshape(RESPONSE_COUNT, RESPONSE_LENGTH, QUERY_HEAD_COUNT * HEAD_SIZE).astype(jnp.bfloat16)


def draw_prompt_keys(key, part):
    key = jax.random.fold_in(key, 12)
    drawn_sample = jnp.clip(jax.random.normal(key, (PROMPT_TOKENS, SHARED_KV_HEADS, HEAD_SIZE), jnp.float32), -5.0, 5.0)
    return drawn_sample.reshape(PROMPT_TOKENS, SHARED_KV_HEADS * HEAD_SIZE).astype(jnp.bfloat16)


def touch_ends(drawn, stream_key, least, high):
    extent = drawn.shape
    spot = [jax.random.randint(jax.random.fold_in(stream_key, axis), (), 0, extent[axis]) for axis in range(len(extent))]
    drawn = drawn.at[tuple(spot)].set(least)
    longest = extent.index(max(extent))
    spot[longest] = (spot[longest] + 1) % extent[longest]
    return drawn.at[tuple(spot)].set(high)


def steps_of(rng, extent, shards, low, high):
    def one(dim, shards_of):
        draws = jax.random.uniform(jax.random.fold_in(jax.random.fold_in(rng, 6), dim), (shards_of,), jnp.float32, low / len(shards), high / len(shards))
        return jnp.repeat(jnp.exp(draws), extent[dim] // shards_of).reshape((-1,) + (1,) * (len(extent) - dim - 1))

    gain = one(*shards[0])
    for cut in shards[1:]:
        gain = gain * one(*cut)
    return gain


def bell_draw(own_key, shape, spread, most, shards=(), held_as=jnp.bfloat16):
    drawn = jax.random.normal(own_key, shape, jnp.float32) * spread
    if len(shards) > 0:
        drawn = steps_of(own_key, shape, shards, -0.22, 0.18) * drawn
    return jnp.clip(drawn, min=-most, max=most).astype(held_as)


def setup_inputs(seed: int = 0, part: int = 0) -> dict:
    key_list = jax.random.split(jax.random.key(seed), 8)
    part_splits = jax.random.split(jax.random.fold_in(key_list[7], part), 8)
    return {
        "queries": draw_queries(jax.random.fold_in(jax.random.fold_in(key_list[7], part), 71), part),
        "response_key_rows": bell_draw(part_splits[1], (RESPONSE_COUNT, RESPONSE_LENGTH, SHARED_KV_HEADS * HEAD_SIZE), 1.0, 6.0, ((0, 16), (1, 8))),
        "response_value_rows": bell_draw(part_splits[2], (RESPONSE_COUNT, RESPONSE_LENGTH, SHARED_KV_HEADS * HEAD_SIZE), 4.0, 24.0, ((0, 16), (1, 8))),
        "prompt_keys": draw_prompt_keys(jax.random.fold_in(jax.random.fold_in(key_list[7], part), 71), part),
        "prompt_value_rows": bell_draw(part_splits[4], (PROMPT_TOKENS, SHARED_KV_HEADS * HEAD_SIZE), 4.0, 24.0, ((0, 128),)),
        "out_grad": bell_draw(part_splits[5], (RESPONSE_COUNT, RESPONSE_LENGTH, QUERY_HEAD_COUNT * HEAD_SIZE), 1.0, 6.0, ((0, 16), (1, 8))),
        "lengths": touch_ends(jax.random.randint(part_splits[6], (RESPONSE_COUNT,), RT, RESPONSE_LENGTH + 1), jax.random.fold_in(part_splits[6], 1), RT, RESPONSE_LENGTH).astype(jnp.int32),
    }


masked_score = -1e30


def attend_head(query_heads, grad_heads, key_rows, value_rows, allowed, live_rows):
    score_scale = key_rows.shape[-1] ** -0.5
    query_f = query_heads.astype(jnp.float32)
    key_f = key_rows.astype(jnp.float32)
    value_f = value_rows.astype(jnp.float32)
    scores = jnp.einsum("tgd,kd->gtk", query_f, key_f) * score_scale
    scores = jnp.where(allowed[None], scores, masked_score)
    row_max = jnp.max(scores, axis=-1, keepdims=True)
    weights = jnp.exp(scores - row_max)
    attn_prob = weights / jnp.sum(weights, axis=-1, keepdims=True)
    prob_half = attn_prob.astype(jnp.bfloat16)
    attended = jnp.einsum("gtk,kd->tgd", prob_half.astype(jnp.float32), value_f)
    attended = jnp.where(live_rows[:, None, None], attended, 0.0).astype(jnp.bfloat16)
    grad_live = jnp.where(live_rows[:, None, None], grad_heads, jnp.zeros_like(grad_heads))
    grad_f = grad_live.astype(jnp.float32)
    row_dot = jnp.sum(grad_f * attended.astype(jnp.float32), axis=-1)
    prob_grad = jnp.einsum("tgd,kd->gtk", grad_f, value_f)
    score_grad = (attn_prob * (prob_grad - row_dot.T[:, :, None])).astype(jnp.bfloat16)
    score_f = score_grad.astype(jnp.float32)
    query_grad = (jnp.einsum("gtk,kd->tgd", score_f, key_f) * score_scale).astype(jnp.bfloat16)
    key_grad = jnp.einsum("gtk,tgd->kd", score_f, query_f) * score_scale
    value_grad = jnp.einsum("gtk,tgd->kd", prob_half.astype(jnp.float32), grad_f)
    return attended, query_grad, key_grad, value_grad


def local_pass(queries, out_grad, key_rows, value_rows, allowed, live_rows):
    row_count = queries.shape[0]
    kv_heads = key_rows.shape[1] // HEAD_SIZE
    group_size = queries.shape[1] // key_rows.shape[1]
    query_heads = queries.reshape(row_count, kv_heads, group_size, HEAD_SIZE).transpose(1, 0, 2, 3)
    grad_heads = out_grad.reshape(row_count, kv_heads, group_size, HEAD_SIZE).transpose(1, 0, 2, 3)
    key_heads = key_rows.reshape(-1, kv_heads, HEAD_SIZE).transpose(1, 0, 2)
    value_heads = value_rows.reshape(-1, kv_heads, HEAD_SIZE).transpose(1, 0, 2)

    def one_head(head_args):
        return attend_head(head_args[0], head_args[1], head_args[2], head_args[3], allowed, live_rows)

    attended, query_grad, key_grad, value_grad = lax.map(one_head, (query_heads, grad_heads, key_heads, value_heads))
    attended = attended.transpose(1, 0, 2, 3).reshape(row_count, -1)
    query_grad = query_grad.transpose(1, 0, 2, 3).reshape(row_count, -1)
    key_grad = key_grad.transpose(1, 0, 2).reshape(key_rows.shape[0], -1)
    value_grad = value_grad.transpose(1, 0, 2).reshape(key_rows.shape[0], -1)
    return attended, query_grad, key_grad, value_grad


def reference(queries, response_key_rows, response_value_rows, prompt_keys, prompt_value_rows, out_grad, lengths):
    width = queries.shape[2]
    prompt_len = prompt_keys.shape[0]
    block_count = RESPONSE_LENGTH // RT

    def block_step(running, block_id):
        resp_id = block_id // block_count
        block = block_id % block_count
        query_block = lax.dynamic_slice(queries, (resp_id, block * RT, jnp.int32(0)), (1, RT, width))[0]
        grad_block = lax.dynamic_slice(out_grad, (resp_id, block * RT, jnp.int32(0)), (1, RT, width))[0]
        own_keys = lax.dynamic_index_in_dim(response_key_rows, resp_id, 0, keepdims=False)
        own_values = lax.dynamic_index_in_dim(response_value_rows, resp_id, 0, keepdims=False)
        key_rows = jnp.concatenate([prompt_keys, own_keys], axis=0)
        value_rows = jnp.concatenate([prompt_value_rows, own_values], axis=0)
        query_pos = block * RT + jnp.arange(RT, dtype=jnp.int32)
        key_pos = jnp.arange(RESPONSE_LENGTH, dtype=jnp.int32)
        causal = key_pos[None, :] <= query_pos[:, None]
        allowed = jnp.concatenate([jnp.full((RT, prompt_len), True), causal], axis=1)
        live_rows = query_pos < lengths[resp_id]
        attended, query_grad, key_grad, value_grad = local_pass(query_block, grad_block, key_rows, value_rows, allowed, live_rows)
        running = (running[0] + key_grad[:prompt_len], running[1] + value_grad[:prompt_len])
        return running, (attended, query_grad, key_grad[prompt_len:].astype(jnp.bfloat16), value_grad[prompt_len:].astype(jnp.bfloat16))

    start = (jnp.zeros(prompt_keys.shape, jnp.float32), jnp.zeros(prompt_keys.shape, jnp.float32))
    block_ids = jnp.arange(RESPONSE_COUNT * block_count, dtype=jnp.int32)
    totals, stacked = lax.scan(block_step, start, block_ids)
    attended = stacked[0].reshape(RESPONSE_COUNT, RESPONSE_LENGTH, width)
    query_grad = stacked[1].reshape(RESPONSE_COUNT, RESPONSE_LENGTH, width)
    kv_width = response_key_rows.shape[2]
    resp_key_grad = jnp.sum(stacked[2].reshape(RESPONSE_COUNT, block_count, RESPONSE_LENGTH, kv_width).astype(jnp.float32), axis=1).astype(jnp.bfloat16)
    resp_value_grad = jnp.sum(stacked[3].reshape(RESPONSE_COUNT, block_count, RESPONSE_LENGTH, kv_width).astype(jnp.float32), axis=1).astype(jnp.bfloat16)
    return attended, query_grad, resp_key_grad, resp_value_grad, totals[0], totals[1]
```

```python
import functools

import jax
import jax.numpy as jnp
from jax import lax
from jax.experimental import pallas as pl
from jax.experimental.pallas import tpu as pltpu
from jax.sharding import PartitionSpec as P

F32 = jnp.float32
BF16 = jnp.bfloat16
MESH = pl.DeviceIdType.MESH

HEADS = 4
GROUP = 8
D = 128
RT = 128
SIDE = 4
CHUNK = 2
SCALE = D**-0.5
SCALE_LOG2E = SCALE * 1.4426950408889634

NT = (((1,), (1,)), ((), ()))
NN = (((1,), (0,)), ((), ()))
TN = (((0,), (0,)), ((), ()))


def dot(a, b, dims):
    return lax.dot_general(a, b, dims, preferred_element_type=F32)


def attend(qs, gs, kp, kr, vp, vr, bias, live):
    sp = dot(qs, kp, NT)
    sr = dot(qs, kr, NT) + bias
    top = jnp.maximum(jnp.max(sp, -1, keepdims=True), jnp.max(sr, -1, keepdims=True))
    top = top * SCALE_LOG2E
    wp = jnp.exp2(sp * SCALE_LOG2E - top)
    wr = jnp.exp2(sr * SCALE_LOG2E - top)
    inv = 1.0 / (jnp.sum(wp, -1, keepdims=True) + jnp.sum(wr, -1, keepdims=True))
    pp = wp * inv
    pr = wr * inv
    php = pp.astype(BF16)
    phr = pr.astype(BF16)
    out = dot(php, vp, NN) + dot(phr, vr, NN)
    out = (out * live).astype(BF16)
    gs = gs * live.astype(BF16)
    row_dot = jnp.sum(gs.astype(F32) * out.astype(F32), -1, keepdims=True)
    dsp = (pp * (dot(gs, vp, NT) - row_dot)).astype(BF16)
    dsr = (pr * (dot(gs, vr, NT) - row_dot)).astype(BF16)
    dq = ((dot(dsp, kp, NN) + dot(dsr, kr, NN)) * SCALE).astype(BF16)
    return out, dq, (dot(dsp, qs, TN), dot(php, gs, TN)), (dot(dsr, qs, TN), dot(phr, gs, TN))


def kernel(
    q_ref, g_ref, kr_ref, vr_ref, pk_ref, pv_ref, len_ref,
    o_ref, dq_ref, drk_ref, drv_ref, dpk_ref, dpv_ref,
    bias, xs, xr, G, RB, AP, AR, T, c0r, c1r, c2r, c3r, d0r, d1r, fin, fr,
    a0_s, a0_r, a1_s, a1_r, a2_s, a2_r, a3_s, a3_r, a4_s, a4_r, b_s, b_r, bs_s, bs_r,
    c0_s, c0_r, c1_s, c1_r, c2_s, c2_r, c3_s, c3_r, c4_s, c4_r, d0_s, d0_r, d1_s, d1_r,
):
    p = lax.axis_index("prompt")
    r = lax.axis_index("resp")
    c = p % 2
    o = 1 - c
    zh = p // 2
    y = r // SIDE
    x = r % SIDE
    sib = {"prompt": zh * 2 + o}

    def z_peer(k):
        return {"prompt": ((zh + k) % SIDE) * 2 + c}

    def y_peer(k):
        return {"resp": ((y + k) % SIDE) * SIDE + x}

    def x_peer(k):
        return {"resp": y * SIDE + (x + k) % SIDE}

    def remote(src, dst, ss, rs, dev):
        return pltpu.make_async_remote_copy(
            src_ref=src, dst_ref=dst, send_sem=ss, recv_sem=rs, device_id=dev, device_id_type=MESH
        )

    peers = [sib] + [f(k) for f in (z_peer, y_peer, x_peer) for k in (1, 2, 3)]
    barrier = pltpu.get_barrier_semaphore()
    for dev in peers:
        pl.semaphore_signal(barrier, inc=1, device_id=dev, device_id_type=MESH)
    mine_k = pk_ref[...].astype(F32)
    mine_v = pv_ref[...].astype(F32)
    is0 = c == 0
    xs[...] = jnp.where(is0, mine_v, mine_k)
    mine = jnp.where(is0, mine_k, mine_v)
    for h in range(HEADS):
        cols = slice(h * D, (h + 1) * D)
        RB[h, 0, p] = kr_ref[:, cols]
        RB[h, 1, p] = vr_ref[:, cols]
    pl.semaphore_wait(barrier, len(peers))

    def a0():
        return remote(xs, xr, a0_s, a0_r, sib)

    def a1(k):
        block = G.at[c, :, zh, y, x]
        return remote(block, block, a1_s.at[k - 1], a1_r.at[k - 1], z_peer(k))

    def a2(h, k):
        block = G.at[c, h, :, y, x]
        dev = {"resp": jnp.where(is0, y_peer(k)["resp"], x_peer(k)["resp"])}
        return remote(block, block, a2_s.at[h, k - 1], a2_r.at[h, k - 1], dev)

    def a3(h, k, core):
        block, dev = (G.at[0, h, :, :, x], x_peer(k)) if core == 0 else (G.at[1, h, :, y], y_peer(k))
        return remote(block, block, a3_s.at[h, k - 1], a3_r.at[h, k - 1], dev)

    def a4(h):
        return remote(G.at[c, h], G.at[c, h], a4_s.at[h], a4_r.at[h], sib)

    def b(h, k):
        return remote(RB.at[h, :, p], RB.at[h, :, p], b_s.at[h, k - 1], b_r.at[h, k - 1], z_peer(k))

    def b_sib(h, k):
        block = RB.at[h, :, ((zh - k + SIDE) % SIDE) * 2 + c]
        return remote(block, block, bs_s.at[h, k], bs_r.at[h, k], sib)

    def c0(h):
        return remote(AP.at[h, o], c0r.at[h], c0_s.at[h], c0_r.at[h], sib)

    def c1(h, k, core):
        if core == 0:
            block, dev = AP.at[h, 0, :, :, (x + k) % SIDE], x_peer(k)
        else:
            block, dev = AP.at[h, 1, :, (y + k) % SIDE], y_peer(k)
        return remote(block, c1r.at[h, k - 1], c1_s.at[h, k - 1], c1_r.at[h, k - 1], dev)

    def c2(h, k):
        to_y = jnp.where(is0, (y + k) % SIDE, y)
        to_x = jnp.where(is0, x, (x + k) % SIDE)
        return remote(
            AP.at[h, c, :, to_y, to_x], c2r.at[h, k - 1], c2_s.at[h, k - 1], c2_r.at[h, k - 1],
            {"resp": to_y * SIDE + to_x},
        )

    def c3(h, k):
        return remote(
            AP.at[h, c, (zh + k) % SIDE, y, x], c3r.at[h, k - 1], c3_s.at[h, k - 1], c3_r.at[h, k - 1], z_peer(k)
        )

    def c4():
        return remote(fin.at[o], fr, c4_s, c4_r, sib)

    def d0(h):
        return remote(T.at[h, :, o], d0r.at[h], d0_s.at[h], d0_r.at[h], sib)

    def d1(h, k):
        to = (zh - k + SIDE) % SIDE
        return remote(T.at[h, to, c], d1r.at[h, k - 1], d1_s.at[h, k - 1], d1_r.at[h, k - 1], {"prompt": to * 2 + c})

    def on_cores(f):
        pl.when(is0)(lambda: f(0))
        pl.when(c == 1)(lambda: f(1))

    def start_b(h):
        b_sib(h, 0).start()
        for k in (1, 2, 3):
            pl.when(zh + k < SIDE)(lambda k=k: b(h, k).start())

    def a2_to_a3(h):
        for k in (1, 2, 3):
            a2(h, k).wait_recv()

        def send(core):
            for k in (1, 2, 3):
                a3(h, k, core).start()

        on_cores(send)

    def relay(h):
        for k in (1, 2, 3):

            def pass_on(k=k):
                b(h, k).wait_recv()
                b_sib(h, k).start()

            pl.when(zh - k >= 0)(pass_on)

        for k in (1, 2, 3):
            a3(h, k, 0).wait_recv()
        a4(h).start()

    def have(h):
        a4(h).wait_recv()
        b_sib(h, 0).wait_recv()
        for k in (1, 2, 3):
            pl.when(zh - k >= 0)(lambda k=k: b_sib(h, k).wait_recv())

    def grads_out(h):
        c0(h).start()
        T[h, :, :, 0] = (AR[0] * SCALE).astype(BF16).reshape(SIDE, 2, RT, D)
        T[h, :, :, 1] = AR[1].astype(BF16).reshape(SIDE, 2, RT, D)
        d0(h).start()

    def step1(h):
        c0(h).wait_recv()
        AP[h, c] += c0r[h]

        def send(core):
            for k in (1, 2, 3):
                c1(h, k, core).start()

        on_cores(send)
        d0(h).wait_recv()
        for k in (1, 2, 3):

            def pair(k=k):
                T[h, zh - k, c] = (T[h, zh - k, c].astype(F32) + d0r[h, zh - k].astype(F32)).astype(BF16)
                d1(h, k).start()

            pl.when(zh - k >= 0)(pair)

    def step2(h):
        for k in (1, 2, 3):
            c1(h, k, 0).wait_recv()
        total = c1r[h, 0] + c1r[h, 1] + c1r[h, 2]

        def add(core):
            if core == 0:
                AP[h, 0, :, :, x] += total
            else:
                AP[h, 1, :, y] += total

        on_cores(add)
        for k in (1, 2, 3):
            c2(h, k).start()

    def step3(h):
        for k in (1, 2, 3):
            c2(h, k).wait_recv()
        AP[h, c, :, y, x] += c2r[h, 0] + c2r[h, 1] + c2r[h, 2]
        for k in (1, 2, 3):
            c3(h, k).start()

    def step4(h):
        for k in (1, 2, 3):
            pl.when(zh + k < SIDE)(lambda k=k: d1(h, k).wait_recv())
        terms = T[h, zh, c].astype(F32) + d0r[h, zh].astype(F32)
        terms = terms + d1r[h, 0].astype(F32) + d1r[h, 1].astype(F32) + d1r[h, 2].astype(F32)
        cols = pl.ds(pl.multiple_of(h * D, D), D)
        drk_ref[:, cols] = terms[0].astype(BF16)
        drv_ref[:, cols] = terms[1].astype(BF16)
        for k in (1, 2, 3):
            c3(h, k).wait_recv()
        total = AP[h, c, zh, y, x] + c3r[h, 0] + c3r[h, 1] + c3r[h, 2]
        total = total * jnp.where(is0, SCALE, 1.0).astype(F32)
        fin[:, :, cols] = total.reshape(2, 8, D)

    a0().start()
    for h in range(HEADS):
        start_b(h)
    for k in (1, 2, 3):

        def clear_b(k=k):
            RB[:, :, pl.ds((zh + k) * 2, 2)] = jnp.zeros((HEADS, 2, 2, RT, D), BF16)

        pl.when(zh + k < SIDE)(clear_b)

        def clear_d(k=k):
            d1r[:, k - 1] = jnp.zeros((HEADS, 2, RT, D), BF16)

        pl.when(zh + k >= SIDE)(clear_d)

    a0().wait_recv()
    theirs = xr[...]
    rows = jnp.concatenate([jnp.where(is0, mine, theirs), jnp.where(is0, theirs, mine)], 0).astype(BF16)
    for h in range(HEADS):
        G[c, h, zh, y, x] = rows[:, h * D : (h + 1) * D]
    for k in (1, 2, 3):
        a1(k).start()
    place = lax.broadcasted_iota(jnp.int32, (RT, SIDE * 2 * RT), 0) + p * RT
    key_place = lax.broadcasted_iota(jnp.int32, (RT, SIDE * 2 * RT), 1)
    bias[...] = jnp.where(key_place <= place, 0.0, -1e30).astype(F32)
    live = (lax.broadcasted_iota(jnp.int32, (RT, 1), 0) + p * RT < len_ref[r]).astype(F32)
    live = jnp.concatenate([live] * CHUNK, 0)
    for k in (1, 2, 3):
        a1(k).wait_recv()
    for h in range(HEADS):
        for k in (1, 2, 3):
            a2(h, k).start()
    for h in range(HEADS):
        a2_to_a3(h)
    relay(0)

    def head(h, _):
        have(h)

        def work(i):
            cols = [pl.ds(pl.multiple_of(h * GROUP * D + (i * CHUNK + j) * D, D), D) for j in range(CHUNK)]
            qs = jnp.concatenate([q_ref[:, col] for col in cols], 0)
            gs = jnp.concatenate([g_ref[:, col] for col in cols], 0)
            mask = jnp.concatenate([bias[...]] * CHUNK, 0)
            kp, vp = (G[t, h].reshape(-1, D) for t in (0, 1))
            kr, vr = (RB[h, t].reshape(-1, D) for t in (0, 1))
            out, dq, prompt_grads, resp_grads = attend(qs, gs, kp, kr, vp, vr, mask, live)
            for j, col in enumerate(cols):
                o_ref[:, col] = out[j * RT : (j + 1) * RT]
                dq_ref[:, col] = dq[j * RT : (j + 1) * RT]
            for t in (0, 1):
                new = prompt_grads[t].reshape(SIDE, SIDE, SIDE, 16, D)
                if i == 0:
                    AP[h, t] = new
                    AR[t] = resp_grads[t]
                else:
                    AP[h, t] += new
                    AR[t] += resp_grads[t]

        work(0)
        pl.when(h > 0)(lambda: step1(h - 1))
        work(1)
        pl.when(h > 0)(lambda: step2(h - 1))
        work(2)
        pl.when(h > 0)(lambda: step3(h - 1))
        pl.when(h < HEADS - 1)(lambda: relay(h + 1))
        work(3)
        grads_out(h)
        pl.when(h > 0)(lambda: step4(h - 1))
        return 0

    lax.fori_loop(0, HEADS, head, 0)
    last = HEADS - 1
    step1(last)
    step2(last)
    step3(last)
    step4(last)
    c4().start()
    c4().wait_recv()
    own = fin[c]
    other = fr[...]
    dpk_ref[...] = jnp.where(is0, own, other)
    dpv_ref[...] = jnp.where(is0, other, own)

    a0().wait_send()
    c4().wait_send()
    for k in (1, 2, 3):
        a1(k).wait_send()

    def sent(h, _):
        a4(h).wait_send()
        c0(h).wait_send()
        d0(h).wait_send()
        b_sib(h, 0).wait_send()
        for k in (1, 2, 3):
            a2(h, k).wait_send()
            a3(h, k, 0).wait_send()
            c1(h, k, 0).wait_send()
            c2(h, k).wait_send()
            c3(h, k).wait_send()

            def conditional(k=k):
                b_sib(h, k).wait_send()
                d1(h, k).wait_send()

            pl.when(zh - k >= 0)(conditional)
            pl.when(zh + k < SIDE)(lambda k=k: b(h, k).wait_send())
        return 0

    lax.fori_loop(0, HEADS, sent, 0)


def body(queries, response_key_rows, response_value_rows, prompt_keys, prompt_value_rows, out_grad, lengths):
    dma = pltpu.SemaphoreType.DMA
    vmem = pl.BlockSpec(memory_space=pltpu.VMEM)
    scratch = [
        pltpu.VMEM((RT, 8 * RT), F32),
        pltpu.VMEM((8, HEADS * D), F32),
        pltpu.VMEM((8, HEADS * D), F32),
        pltpu.VMEM((2, HEADS, SIDE, SIDE, SIDE, 16, D), BF16),
        pltpu.VMEM((HEADS, 2, 8, RT, D), BF16),
        pltpu.VMEM((HEADS, 2, SIDE, SIDE, SIDE, 16, D), F32),
        pltpu.VMEM((2, 8 * RT, D), F32),
        pltpu.VMEM((HEADS, SIDE, 2, 2, RT, D), BF16),
        pltpu.VMEM((HEADS, SIDE, SIDE, SIDE, 16, D), F32),
        pltpu.VMEM((HEADS, 3, SIDE, SIDE, 16, D), F32),
        pltpu.VMEM((HEADS, 3, SIDE, 16, D), F32),
        pltpu.VMEM((HEADS, 3, 16, D), F32),
        pltpu.VMEM((HEADS, SIDE, 2, RT, D), BF16),
        pltpu.VMEM((HEADS, 3, 2, RT, D), BF16),
        pltpu.VMEM((2, 8, HEADS * D), F32),
        pltpu.VMEM((8, HEADS * D), F32),
    ]
    per_peer = dma((HEADS, 3))
    per_head = dma((HEADS,))
    sems = [dma, dma, dma((3,)), dma((3,)), per_peer, per_peer, per_peer, per_peer, per_head, per_head]
    sems += [per_peer, per_peer, dma((HEADS, 4)), dma((HEADS, 4))]
    sems += [per_head, per_head] + [per_peer] * 6 + [dma, dma, per_head, per_head, per_peer, per_peer]
    wide = jax.ShapeDtypeStruct(queries.shape[1:], BF16)
    rows = jax.ShapeDtypeStruct(response_key_rows.shape[1:], BF16)
    shared = jax.ShapeDtypeStruct(prompt_keys.shape, F32)
    out, dq, drk, drv, dpk, dpv = pl.pallas_call(
        kernel,
        out_shape=[wide, wide, rows, rows, shared, shared],
        in_specs=[vmem] * 6 + [pl.BlockSpec(memory_space=pltpu.SMEM)],
        out_specs=[vmem] * 6,
        scratch_shapes=scratch + sems,
        compiler_params=pltpu.CompilerParams(
            collective_id=0, has_side_effects=True, vmem_limit_bytes=56 * 2**20
        ),
        cost_estimate=pl.CostEstimate(flops=13 * 10**9, bytes_accessed=5 * 2**20, transcendentals=2**23),
    )(queries[0], out_grad[0], response_key_rows[0], response_value_rows[0], prompt_keys, prompt_value_rows, lengths)
    return out[None], dq[None], drk[None], drv[None], dpk, dpv


def solution(mesh):
    rows = P(("grp", "resp"), "prompt", None)
    shared = P(("grp", "prompt", "resp"), None)
    return jax.shard_map(
        body,
        mesh=mesh,
        in_specs=(rows, rows, rows, shared, shared, rows, P("grp")),
        out_specs=(rows, rows, rows, rows, shared, shared),
        check_vma=False,
    )
```

```python
import functools

import jax
import jax.numpy as jnp
from jax import lax
from jax.experimental import pallas as pl
from jax.experimental.pallas import tpu as pltpu
from jax.sharding import PartitionSpec as P

F32 = jnp.float32
BF16 = jnp.bfloat16
MESH = pl.DeviceIdType.MESH

HEADS = 4
GROUP = 8
D = 128
RT = 128
SIDE = 4
CHUNK = 4
SCALE = D**-0.5
SCALE_LOG2E = SCALE * 1.4426950408889634

NT = (((1,), (1,)), ((), ()))
NN = (((1,), (0,)), ((), ()))
TN = (((0,), (0,)), ((), ()))


def dot(a, b, dims):
    return lax.dot_general(a, b, dims, preferred_element_type=F32)


def kernel(
    q_ref, g_ref, kr_ref, vr_ref, pk_ref, pv_ref, len_ref,
    o_ref, dq_ref, drk_ref, drv_ref, dpk_ref, dpv_ref,
    q_buf, g_buf, q_sem, g_sem, KT, VT, DS, bias, xs, xr, G, RB, AP, AR, T, c0r, c1r, c2r, c3r, d0r, d1r, fin, fr,
    a0_s, a0_r, a1_s, a1_r, a2_s, a2_r, a3_s, a3_r, a4_s, a4_r, b_s, b_r, bs_s, bs_r,
    c0_s, c0_r, c1_s, c1_r, c2_s, c2_r, c3_s, c3_r, c4_s, c4_r, d0_s, d0_r, d1_s, d1_r,
):
    p = lax.axis_index("prompt")
    r = lax.axis_index("resp")
    c = p % 2
    o = 1 - c
    zh = p // 2
    y = r // SIDE
    x = r % SIDE
    sib = {"prompt": zh * 2 + o}

    def z_peer(k):
        return {"prompt": ((zh + k) % SIDE) * 2 + c}

    def y_peer(k):
        return {"resp": ((y + k) % SIDE) * SIDE + x}

    def x_peer(k):
        return {"resp": y * SIDE + (x + k) % SIDE}

    def remote(src, dst, ss, rs, dev):
        return pltpu.make_async_remote_copy(
            src_ref=src, dst_ref=dst, send_sem=ss, recv_sem=rs, device_id=dev, device_id_type=MESH
        )

    peers = [sib] + [f(k) for f in (z_peer, y_peer, x_peer) for k in (1, 2, 3)]
    barrier = pltpu.get_barrier_semaphore()
    for dev in peers:
        pl.semaphore_signal(barrier, inc=1, device_id=dev, device_id_type=MESH)
    mine_k = pk_ref[...].astype(F32)
    mine_v = pv_ref[...].astype(F32)
    is0 = c == 0
    xs[...] = jnp.where(is0, mine_v, mine_k)
    mine = jnp.where(is0, mine_k, mine_v)
    for h in range(HEADS):
        cols = slice(h * D, (h + 1) * D)
        RB[h, 0, p] = kr_ref[:, cols]
        RB[h, 1, p] = vr_ref[:, cols]
    pl.semaphore_wait(barrier, len(peers))

    def a0():
        return remote(xs, xr, a0_s, a0_r, sib)

    def a1(k):
        block = G.at[c, :, zh, y, x]
        return remote(block, block, a1_s.at[k - 1], a1_r.at[k - 1], z_peer(k))

    def a2(h, k):
        block = G.at[c, h, :, y, x]
        dev = {"resp": jnp.where(is0, y_peer(k)["resp"], x_peer(k)["resp"])}
        return remote(block, block, a2_s.at[h, k - 1], a2_r.at[h, k - 1], dev)

    def a3(h, k, core):
        block, dev = (G.at[0, h, :, :, x], x_peer(k)) if core == 0 else (G.at[1, h, :, y], y_peer(k))
        return remote(block, block, a3_s.at[h, k - 1], a3_r.at[h, k - 1], dev)

    def a4(h):
        return remote(G.at[c, h], G.at[c, h], a4_s.at[h], a4_r.at[h], sib)

    def b(h, k):
        return remote(RB.at[h, :, p], RB.at[h, :, p], b_s.at[h, k - 1], b_r.at[h, k - 1], z_peer(k))

    def b_sib(h, k):
        block = RB.at[h, :, ((zh - k + SIDE) % SIDE) * 2 + c]
        return remote(block, block, bs_s.at[h, k], bs_r.at[h, k], sib)

    def c0(h):
        return remote(AP.at[h, o], c0r.at[h], c0_s.at[h], c0_r.at[h], sib)

    def c1(h, k, core):
        if core == 0:
            block, dev = AP.at[h, 0, :, :, (x + k) % SIDE], x_peer(k)
        else:
            block, dev = AP.at[h, 1, :, (y + k) % SIDE], y_peer(k)
        return remote(block, c1r.at[h, k - 1], c1_s.at[h, k - 1], c1_r.at[h, k - 1], dev)

    def c2(h, k):
        to_y = jnp.where(is0, (y + k) % SIDE, y)
        to_x = jnp.where(is0, x, (x + k) % SIDE)
        return remote(
            AP.at[h, c, :, to_y, to_x], c2r.at[h, k - 1], c2_s.at[h, k - 1], c2_r.at[h, k - 1],
            {"resp": to_y * SIDE + to_x},
        )

    def c3(h, k):
        return remote(
            AP.at[h, c, (zh + k) % SIDE, y, x], c3r.at[h, k - 1], c3_s.at[h, k - 1], c3_r.at[h, k - 1], z_peer(k)
        )

    def c4():
        return remote(fin.at[o], fr, c4_s, c4_r, sib)

    def d0(h):
        return remote(T.at[h, :, o], d0r.at[h], d0_s.at[h], d0_r.at[h], sib)

    def d1(h, k):
        to = (zh - k + SIDE) % SIDE
        return remote(T.at[h, to, c], d1r.at[h, k - 1], d1_s.at[h, k - 1], d1_r.at[h, k - 1], {"prompt": to * 2 + c})

    def on_cores(f):
        pl.when(is0)(lambda: f(0))
        pl.when(c == 1)(lambda: f(1))

    def start_b(h):
        b_sib(h, 0).start()
        for k in (1, 2, 3):
            pl.when(zh + k < SIDE)(lambda k=k: b(h, k).start())

    def a2_to_a3(h):
        for k in (1, 2, 3):
            a2(h, k).wait_recv()

        def send(core):
            for k in (1, 2, 3):
                a3(h, k, core).start()

        on_cores(send)

    def relay(h):
        for k in (1, 2, 3):
            a3(h, k, 0).wait_recv()
        a4(h).start()
        for k in (1, 2, 3):

            def pass_on(k=k):
                b(h, k).wait_recv()
                b_sib(h, k).start()

            pl.when(zh - k >= 0)(pass_on)

    def have_resp(h):
        b_sib(h, 0).wait_recv()
        for k in (1, 2, 3):
            pl.when(zh - k >= 0)(lambda k=k: b_sib(h, k).wait_recv())

    def terms_out(h):
        T[h, :, :, 0] = (AR[0] * SCALE).astype(BF16).reshape(SIDE, 2, RT, D)
        T[h, :, :, 1] = AR[1].astype(BF16).reshape(SIDE, 2, RT, D)
        d0(h).start()

    def step1(h):
        step1_prompt(h)
        step1_resp(h)

    def step1_prompt(h):
        c0(h).wait_recv()
        AP[h, c] += c0r[h]

        def send(core):
            for k in (1, 2, 3):
                c1(h, k, core).start()

        on_cores(send)

    def step1_resp(h):
        d0(h).wait_recv()
        for k in (1, 2, 3):

            def pair(k=k):
                T[h, zh - k, c] = (T[h, zh - k, c].astype(F32) + d0r[h, zh - k].astype(F32)).astype(BF16)
                d1(h, k).start()

            pl.when(zh - k >= 0)(pair)

    def step2(h):
        for k in (1, 2, 3):
            c1(h, k, 0).wait_recv()
        total = c1r[h, 0] + c1r[h, 1] + c1r[h, 2]

        def add(core):
            if core == 0:
                AP[h, 0, :, :, x] += total
            else:
                AP[h, 1, :, y] += total

        on_cores(add)
        for k in (1, 2, 3):
            c2(h, k).start()

    def step3(h):
        for k in (1, 2, 3):
            c2(h, k).wait_recv()
        AP[h, c, :, y, x] += c2r[h, 0] + c2r[h, 1] + c2r[h, 2]
        for k in (1, 2, 3):
            c3(h, k).start()

    def step4(h):
        for k in (1, 2, 3):
            pl.when(zh + k < SIDE)(lambda k=k: d1(h, k).wait_recv())
        terms = T[h, zh, c].astype(F32) + d0r[h, zh].astype(F32)
        terms = terms + d1r[h, 0].astype(F32) + d1r[h, 1].astype(F32) + d1r[h, 2].astype(F32)
        cols = pl.ds(pl.multiple_of(h * D, D), D)
        drk_ref[:, cols] = terms[0].astype(BF16)
        drv_ref[:, cols] = terms[1].astype(BF16)
        for k in (1, 2, 3):
            c3(h, k).wait_recv()
        total = AP[h, c, zh, y, x] + c3r[h, 0] + c3r[h, 1] + c3r[h, 2]
        total = total * jnp.where(is0, SCALE, 1.0).astype(F32)
        fin[:, :, cols] = total.reshape(2, 8, D)

    a0().start()
    q_in = pltpu.make_async_copy(q_ref, q_buf, q_sem)
    g_in = pltpu.make_async_copy(g_ref, g_buf, g_sem)
    q_in.start()
    g_in.start()
    for k in (1, 2, 3):

        def clear_b(k=k):
            RB[:, :, pl.ds((zh + k) * 2, 2)] = jnp.zeros((HEADS, 2, 2, RT, D), BF16)

        pl.when(zh + k < SIDE)(clear_b)

        def clear_d(k=k):
            d1r[:, k - 1] = jnp.zeros((HEADS, 2, RT, D), BF16)

        pl.when(zh + k >= SIDE)(clear_d)

    a0().wait_recv()
    theirs = xr[...]
    rows = jnp.concatenate([jnp.where(is0, mine, theirs), jnp.where(is0, theirs, mine)], 0).astype(BF16)
    for h in range(HEADS):
        G[c, h, zh, y, x] = rows[:, h * D : (h + 1) * D]
    for k in (1, 2, 3):
        a1(k).start()
    start_b(0)
    place = lax.broadcasted_iota(jnp.int32, (SIDE * 2 * RT, RT), 1) + p * RT
    key_place = lax.broadcasted_iota(jnp.int32, (SIDE * 2 * RT, RT), 0)
    bias[...] = jnp.where(key_place <= place, 0.0, -1e30).astype(F32)
    length = len_ref[r]
    live = (lax.broadcasted_iota(jnp.int32, (RT, 1), 0) + p * RT < length).astype(F32).astype(BF16)
    live = jnp.concatenate([live] * CHUNK, 0)
    live_cols = (lax.broadcasted_iota(jnp.int32, (1, RT), 1) + p * RT < length).astype(F32)
    live_cols = jnp.concatenate([live_cols] * CHUNK, 1)
    for k in (1, 2, 3):
        a1(k).wait_recv()
    for k in (1, 2, 3):
        a2(0, k).start()
    a2_to_a3(0)
    for h in range(1, HEADS):
        for k in (1, 2, 3):
            a2(h, k).start()
    q_in.wait()
    g_in.wait()
    relay(0)
    for h in range(1, HEADS):
        a2_to_a3(h)
    start_b(1)

    def dq_part(h, i):
        for_rows = dot(KT[h], DS[h % 2, i], NN) * SCALE
        for j in range(CHUNK):
            col = pl.ds(pl.multiple_of(h * GROUP * D + (i * CHUNK + j) * D, D), D)
            dq_ref[:, col] = for_rows[:, j * RT : (j + 1) * RT].T.astype(BF16)

    def head(h, _):
        keys = SIDE * 2 * RT
        a4(h).wait_recv()
        kp, vp = (G[t, h].reshape(-1, D) for t in (0, 1))
        KT[h, :, :keys] = kp.T
        VT[:, :keys] = vp.T

        def tick(n):
            if n == 0:
                pl.when(h > 0)(lambda: step1(h - 1))
                pl.when(h < HEADS - 2)(lambda: start_b(h + 2))
            if n == 1:
                pl.when(h > 1)(lambda: step3(h - 2))
                pl.when(h < HEADS - 1)(lambda: relay(h + 1))
            if n == 2:
                pl.when(h > 2)(lambda: step4(h - 3))
            if n == 3:
                pl.when(h > 0)(lambda: step2(h - 1))

        for i in range(GROUP // CHUNK):
            cols = [pl.ds(pl.multiple_of(h * GROUP * D + (i * CHUNK + j) * D, D), D) for j in range(CHUNK)]
            qs = jnp.concatenate([q_buf[:, col] for col in cols], 0)
            gs = jnp.concatenate([g_buf[:, col] for col in cols], 0) * live
            sp = dot(kp, qs, NT)
            dpp = dot(vp, gs, NT)
            if i == 0:
                have_resp(h)
            kr, vr = (RB[h, t].reshape(-1, D) for t in (0, 1))
            if i == 0:
                KT[h, :, keys:] = kr.T
                VT[:, keys:] = vr.T
            sr = dot(kr, qs, NT) + jnp.concatenate([bias[...]] * CHUNK, 1)
            dpr = dot(vr, gs, NT)
            top = jnp.maximum(jnp.max(sp, 0, keepdims=True), jnp.max(sr, 0, keepdims=True))
            top = top * SCALE_LOG2E
            wp = jnp.exp2(sp * SCALE_LOG2E - top)
            wr = jnp.exp2(sr * SCALE_LOG2E - top)
            inv = 1.0 / (jnp.sum(wp, 0, keepdims=True) + jnp.sum(wr, 0, keepdims=True))
            pp = wp * inv
            pr = wr * inv
            php = pp.astype(BF16)
            phr = pr.astype(BF16)
            out = dot(VT[:, :keys], php, NN) + dot(VT[:, keys:], phr, NN)
            out = (out * live_cols).astype(BF16).astype(F32)
            for j, col in enumerate(cols):
                o_ref[:, col] = out[:, j * RT : (j + 1) * RT].T.astype(BF16)
            row_dot = jnp.sum(gs.astype(F32).T * out, 0, keepdims=True)
            tick(2 * i)
            dsp = (pp * (dpp - row_dot)).astype(BF16)
            dsr = (pr * (dpr - row_dot)).astype(BF16)
            DS[h % 2, i, :keys] = dsp
            DS[h % 2, i, keys:] = dsr
            for t, new in ((0, dot(dsp, qs, NN)), (1, dot(php, gs, NN))):
                new = new.reshape(SIDE, SIDE, SIDE, 16, D)
                if i == 0:
                    AP[h, t] = new
                else:
                    AP[h, t] += new
            if i == GROUP // CHUNK - 1:
                c0(h).start()
            for t, new in ((0, dot(dsr, qs, NN)), (1, dot(phr, gs, NN))):
                if i == 0:
                    AR[t] = new
                else:
                    AR[t] += new
            if i == GROUP // CHUNK - 1:
                terms_out(h)
            tick(2 * i + 1)

        def dq_now():
            for i in range(GROUP // CHUNK):
                dq_part(h, i)

        pl.when(h < 2)(dq_now)
        return 0

    lax.fori_loop(0, HEADS, head, 0)
    dq_part(2, 0)
    step1_prompt(3)
    dq_part(2, 1)
    step1_resp(3)
    step3(2)
    dq_part(3, 0)
    dq_part(3, 1)
    step4(1)
    step4(2)
    step2(3)
    step3(3)
    step4(3)
    c4().start()
    c4().wait_recv()
    own = fin[c]
    other = fr[...]
    dpk_ref[...] = jnp.where(is0, own, other)
    dpv_ref[...] = jnp.where(is0, other, own)

    a0().wait_send()
    c4().wait_send()
    for k in (1, 2, 3):
        a1(k).wait_send()

    def sent(h, _):
        a4(h).wait_send()
        c0(h).wait_send()
        d0(h).wait_send()
        b_sib(h, 0).wait_send()
        for k in (1, 2, 3):
            a2(h, k).wait_send()
            a3(h, k, 0).wait_send()
            c1(h, k, 0).wait_send()
            c2(h, k).wait_send()
            c3(h, k).wait_send()

            def conditional(k=k):
                b_sib(h, k).wait_send()
                d1(h, k).wait_send()

            pl.when(zh - k >= 0)(conditional)
            pl.when(zh + k < SIDE)(lambda k=k: b(h, k).wait_send())
        return 0

    lax.fori_loop(0, HEADS, sent, 0)


def hand_over(*refs):
    n = (len(refs) - 1) // 2
    copies = [pltpu.make_async_copy(refs[i], refs[n + i], refs[-1].at[i]) for i in range(n)]
    for copy in copies:
        copy.start()
    for copy in copies:
        copy.wait()


def body(queries, response_key_rows, response_value_rows, prompt_keys, prompt_value_rows, out_grad, lengths):
    dma = pltpu.SemaphoreType.DMA
    vmem = pl.BlockSpec(memory_space=pltpu.VMEM)
    hbm = pl.BlockSpec(memory_space=pl.ANY)
    scratch = [
        pltpu.VMEM((RT, HEADS * GROUP * D), BF16),
        pltpu.VMEM((RT, HEADS * GROUP * D), BF16),
        dma,
        dma,
        pltpu.VMEM((HEADS, D, 16 * RT), BF16),
        pltpu.VMEM((D, 16 * RT), BF16),
        pltpu.VMEM((2, GROUP // CHUNK, 16 * RT, CHUNK * RT), BF16),
        pltpu.VMEM((8 * RT, RT), F32),
        pltpu.VMEM((8, HEADS * D), F32),
        pltpu.VMEM((8, HEADS * D), F32),
        pltpu.VMEM((2, HEADS, SIDE, SIDE, SIDE, 16, D), BF16),
        pltpu.VMEM((HEADS, 2, 8, RT, D), BF16),
        pltpu.VMEM((HEADS, 2, SIDE, SIDE, SIDE, 16, D), F32),
        pltpu.VMEM((2, 8 * RT, D), F32),
        pltpu.VMEM((HEADS, SIDE, 2, 2, RT, D), BF16),
        pltpu.VMEM((HEADS, SIDE, SIDE, SIDE, 16, D), F32),
        pltpu.VMEM((HEADS, 3, SIDE, SIDE, 16, D), F32),
        pltpu.VMEM((HEADS, 3, SIDE, 16, D), F32),
        pltpu.VMEM((HEADS, 3, 16, D), F32),
        pltpu.VMEM((HEADS, SIDE, 2, RT, D), BF16),
        pltpu.VMEM((HEADS, 3, 2, RT, D), BF16),
        pltpu.VMEM((2, 8, HEADS * D), F32),
        pltpu.VMEM((8, HEADS * D), F32),
    ]
    per_peer = dma((HEADS, 3))
    per_head = dma((HEADS,))
    sems = [dma, dma, dma((3,)), dma((3,)), per_peer, per_peer, per_peer, per_peer, per_head, per_head]
    sems += [per_peer, per_peer, dma((HEADS, 4)), dma((HEADS, 4))]
    sems += [per_head, per_head] + [per_peer] * 6 + [dma, dma, per_head, per_head, per_peer, per_peer]
    wide = jax.ShapeDtypeStruct(queries.shape[1:], BF16)
    rows = jax.ShapeDtypeStruct(response_key_rows.shape[1:], BF16)
    shared = jax.ShapeDtypeStruct(prompt_keys.shape, F32)
    shapes = [wide, wide, rows, rows, shared, shared]
    results = pl.pallas_call(
        kernel,
        out_shape=shapes,
        in_specs=[hbm] * 2 + [vmem] * 4 + [pl.BlockSpec(memory_space=pltpu.SMEM)],
        out_specs=[vmem] * 6,
        scratch_shapes=scratch + sems,
        compiler_params=pltpu.CompilerParams(
            collective_id=0, has_side_effects=True, vmem_limit_bytes=60 * 2**20
        ),
        cost_estimate=pl.CostEstimate(flops=13 * 10**9, bytes_accessed=5 * 2**20, transcendentals=2**23),
    )(queries[0], out_grad[0], response_key_rows[0], response_value_rows[0], prompt_keys, prompt_value_rows, lengths)
    out, dq, drk, drv, dpk, dpv = pl.pallas_call(
        hand_over,
        out_shape=shapes,
        in_specs=[vmem] * 6,
        out_specs=[hbm] * 6,
        scratch_shapes=[dma((6,))],
    )(*results)
    return out[None], dq[None], drk[None], drv[None], dpk, dpv


def solution(mesh):
    rows = P(("grp", "resp"), "prompt", None)
    shared = P(("grp", "prompt", "resp"), None)
    return jax.shard_map(
        body,
        mesh=mesh,
        in_specs=(rows, rows, rows, shared, shared, rows, P("grp")),
        out_specs=(rows, rows, rows, rows, shared, shared),
        check_vma=False,
    )
```

```python
import functools

import jax
import jax.numpy as jnp
from jax import lax
from jax.experimental import pallas as pl
from jax.experimental.pallas import tpu as pltpu
from jax.sharding import PartitionSpec as P

F32 = jnp.float32
BF16 = jnp.bfloat16
MESH = pl.DeviceIdType.MESH

HEADS = 4
GROUP = 8
D = 128
RT = 128
SIDE = 4
PLANE = 16
SLOTS = 4
TILE = 256
KEYS = 1024
SCALE = D**-0.5
SCALE_LOG2E = SCALE * 1.4426950408889634

NT = (((1,), (1,)), ((), ()))
NN = (((1,), (0,)), ((), ()))
TN = (((0,), (0,)), ((), ()))


def dot(a, b, dims):
    return lax.dot_general(a, b, dims, preferred_element_type=F32)


def kernel(
    q_ref, g_ref, kr_ref, vr_ref, pk_ref, pv_ref, len_ref,
    o_ref, dq_ref, drk_ref, drv_ref, dpk_ref, dpv_ref,
    q_buf, g_buf, q_sem, g_sem, KV, KT, VT, DS, bias, G, RB, AP, T, c0r, c1r, c2r, d0r, d1r,
    a1_s, a1_r, a2_s, a2_r, a3_s, a3_r, b_s, b_r, bs_s, bs_r,
    c0_s, c0_r, c1_s, c1_r, c2_s, c2_r, d0_s, d0_r, d1_s, d1_r,
):
    p = lax.axis_index("prompt")
    r = lax.axis_index("resp")
    c = p % 2
    o = 1 - c
    zh = p // 2
    sib = {"prompt": zh * 2 + o}

    def z_peer(k):
        return {"prompt": ((zh + k) % SIDE) * 2 + c}

    def plane_peer(j):
        return {"resp": (r + j) % PLANE}

    def remote(src, dst, ss, rs, dev):
        return pltpu.make_async_remote_copy(
            src_ref=src, dst_ref=dst, send_sem=ss, recv_sem=rs, device_id=dev, device_id_type=MESH
        )

    peers = [sib] + [z_peer(k) for k in (1, 2, 3)] + [plane_peer(j) for j in range(1, PLANE)]
    barrier = pltpu.get_barrier_semaphore()
    for dev in peers:
        pl.semaphore_signal(barrier, inc=1, device_id=dev, device_id_type=MESH)
    mine = jnp.concatenate([pk_ref[...].astype(F32), pv_ref[...].astype(F32)], 0).astype(BF16)
    for h in range(HEADS):
        cols = slice(h * D, (h + 1) * D)
        RB[h, 0, p] = kr_ref[:, cols]
        RB[h, 1, p] = vr_ref[:, cols]
        G[c, h, r, zh] = mine[:, cols]
    pl.semaphore_wait(barrier, len(peers))

    def a1(part, k):
        block = G.at[c, 0:1, r, zh] if part == 0 else G.at[c, 1:HEADS, r, zh]
        return remote(block, block, a1_s.at[part, k - 1], a1_r.at[part, k - 1], z_peer(k))

    def a2_start(h):
        def send(j, _):
            remote(G.at[c, h, r], G.at[c, h, r], a2_s.at[h], a2_r.at[h], plane_peer(j)).start()
            return 0

        lax.fori_loop(1, PLANE, send, 0)

    def a2_all(h):
        rows = G.at[c, h, 0 : PLANE - 1]
        return remote(rows, rows, a2_s.at[h], a2_r.at[h], sib)

    def a3(h):
        return remote(G.at[c, h], G.at[c, h], a3_s.at[h], a3_r.at[h], sib)

    def b(h, t, k):
        return remote(RB.at[h, t, p], RB.at[h, t, p], b_s.at[h, t, k - 1], b_r.at[h, t, k - 1], z_peer(k))

    def b_sib(h, t, k):
        block = RB.at[h, t, ((zh - k + SIDE) % SIDE) * 2 + c]
        return remote(block, block, bs_s.at[h, t, k], bs_r.at[h, t, k], sib)

    def c0(h):
        return remote(AP.at[h, o], c0r.at[h], c0_s.at[h], c0_r.at[h], sib)

    def c1_start(h):
        def send(j, _):
            to = (r + j) % PLANE
            remote(AP.at[h, c, :, to], c1r.at[h, j - 1], c1_s.at[h], c1_r.at[h], {"resp": to}).start()
            return 0

        lax.fori_loop(1, PLANE, send, 0)

    def c1_all(h):
        return remote(c1r.at[h], c1r.at[h], c1_s.at[h], c1_r.at[h], sib)

    def c2(h, k):
        to = (zh + k) % SIDE
        return remote(AP.at[h, c, :, r, to], c2r.at[h, k - 1], c2_s.at[h, k - 1], c2_r.at[h, k - 1], z_peer(k))

    def d0(h):
        return remote(T.at[h, :, o], d0r.at[h], d0_s.at[h], d0_r.at[h], sib)

    def d1(h, k):
        to = (zh - k + SIDE) % SIDE
        return remote(T.at[h, to, c], d1r.at[h, k - 1], d1_s.at[h, k - 1], d1_r.at[h, k - 1], {"prompt": to * 2 + c})

    def start_b(h):
        for t in (0, 1):
            b_sib(h, t, 0).start()
            for k in (1, 2, 3):
                pl.when(zh + k < SIDE)(lambda t=t, k=k: b(h, t, k).start())

    def relay_prompt(h):
        a2_all(h).wait_recv()
        a3(h).start()

    def relay_resp(h, t):
        for k in (1, 2, 3):

            def pass_on(k=k):
                b(h, t, k).wait_recv()
                b_sib(h, t, k).start()

            pl.when(zh - k >= 0)(pass_on)

    def have_resp(h, t):
        b_sib(h, t, 0).wait_recv()
        for k in (1, 2, 3):
            pl.when(zh - k >= 0)(lambda k=k: b_sib(h, t, k).wait_recv())

    def step1(h):
        step1_prompt(h)
        step1_resp(h)

    def step1_prompt(h):
        c0(h).wait_recv()
        AP[h, c] += c0r[h]
        c1_start(h)

    def step1_resp(h):
        d0(h).wait_recv()
        for k in (1, 2, 3):

            def pair(k=k):
                T[h, zh - k, c] = (T[h, zh - k, c].astype(F32) + d0r[h, zh - k].astype(F32)).astype(BF16)
                d1(h, k).start()

            pl.when(zh - k >= 0)(pair)

    def step2(h):
        c1_all(h).wait_recv()
        total = AP[h, c, :, r]
        for j in range(PLANE - 1):
            total = total + c1r[h, j]
        AP[h, c, :, r] = total
        for k in (1, 2, 3):
            c2(h, k).start()

    def step3(h):
        for k in (1, 2, 3):
            pl.when(zh + k < SIDE)(lambda k=k: d1(h, k).wait_recv())
        terms = T[h, zh, c].astype(F32) + d0r[h, zh].astype(F32)
        terms = terms + d1r[h, 0].astype(F32) + d1r[h, 1].astype(F32) + d1r[h, 2].astype(F32)
        cols = pl.ds(pl.multiple_of(h * D, D), D)
        drk_ref[:, cols] = terms[0].astype(BF16)
        drv_ref[:, cols] = terms[1].astype(BF16)
        for k in (1, 2, 3):
            c2(h, k).wait_recv()
        total = AP[h, c, :, r, zh] + c2r[h, 0] + c2r[h, 1] + c2r[h, 2]
        dpk_ref[:, cols] = total[0] * SCALE
        dpv_ref[:, cols] = total[1]

    for part in (0, 1):
        for k in (1, 2, 3):
            a1(part, k).start()
    start_b(0)
    q_in = pltpu.make_async_copy(q_ref, q_buf, q_sem)
    g_in = pltpu.make_async_copy(g_ref, g_buf, g_sem)
    q_in.start()
    g_in.start()
    for k in (1, 2, 3):
        a1(0, k).wait_recv()
    a2_start(0)
    for k in (1, 2, 3):

        def clear_b(k=k):
            RB[:, :, pl.ds((zh + k) * 2, 2)] = jnp.zeros((HEADS, 2, 2, RT, D), BF16)

        pl.when(zh + k < SIDE)(clear_b)

        def clear_d(k=k):
            d1r[:, k - 1] = jnp.zeros((HEADS, 2, RT, D), BF16)

        pl.when(zh + k >= SIDE)(clear_d)

    for k in (1, 2, 3):
        a1(1, k).wait_recv()
    for h in range(1, HEADS):
        a2_start(h)
    place = lax.broadcasted_iota(jnp.int32, (SIDE * 2 * RT, RT), 1) + p * RT
    key_place = lax.broadcasted_iota(jnp.int32, (SIDE * 2 * RT, RT), 0)
    bias[...] = jnp.where(key_place <= place, 0.0, -1e30).astype(F32)
    length = len_ref[r]
    live = (lax.broadcasted_iota(jnp.int32, (RT, 1), 0) + p * RT < length).astype(F32).astype(BF16)
    live = jnp.concatenate([live] * GROUP, 0)
    live_cols = (lax.broadcasted_iota(jnp.int32, (1, RT), 1) + p * RT < length).astype(F32)
    live_cols = jnp.concatenate([live_cols] * GROUP, 1)
    q_in.wait()
    g_in.wait()
    relay_prompt(0)
    relay_resp(0, 0)
    start_b(1)

    def dq_part(h):
        for_rows = dot(KT[h], DS[h % SLOTS], NN) * SCALE
        for j in range(GROUP):
            col = pl.ds(pl.multiple_of((h * GROUP + j) * D, D), D)
            dq_ref[:, col] = for_rows[:, j * RT : (j + 1) * RT].T.astype(BF16)

    def head(h, _):
        a3(h).wait_recv()
        for lane in (0, 1):
            rows = slice(lane * KEYS // 2, (lane + 1) * KEYS // 2)
            blocks = G[lane, h].astype(F32).reshape(PLANE * SIDE, 2, 8, D)
            KV[0, rows] = blocks[:, 0].reshape(-1, D).astype(BF16)
            KV[1, rows] = blocks[:, 1].reshape(-1, D).astype(BF16)
        kp, vp = KV[0], KV[1]
        KT[h, :, :KEYS] = kp.T
        VT[:, :KEYS] = vp.T
        cols = [pl.ds(pl.multiple_of((h * GROUP + j) * D, D), D) for j in range(GROUP)]
        qs = jnp.concatenate([q_buf[:, col] for col in cols], 0)
        gs = jnp.concatenate([g_buf[:, col] for col in cols], 0) * live

        tiles = [slice(first, first + TILE) for first in range(0, KEYS, TILE)]
        scores = [dot(kp[tile], qs, NT) for tile in tiles]
        top = functools.reduce(jnp.maximum, [jnp.max(score, 0, keepdims=True) for score in scores])
        have_resp(h, 0)
        kr = RB[h, 0].reshape(-1, D)
        KT[h, :, KEYS:] = kr.T
        for tile in tiles:
            score = dot(kr[tile], qs, NT) + jnp.concatenate([bias[tile]] * GROUP, 1)
            top = jnp.maximum(top, jnp.max(score, 0, keepdims=True))
            scores.append(score)
        pl.when(h > 0)(lambda: step1(h - 1))
        pl.when(h == 0)(lambda: relay_resp(h, 1))
        pl.when(h < HEADS - 2)(lambda: start_b(h + 2))
        top = top * SCALE_LOG2E
        weights = [jnp.exp2(score * SCALE_LOG2E - top) for score in scores]
        inv = 1.0 / functools.reduce(jnp.add, [jnp.sum(weight, 0, keepdims=True) for weight in weights])

        def after_weights():
            relay_prompt(h + 1)
            relay_resp(h + 1, 0)
            relay_resp(h + 1, 1)

        pl.when(h < HEADS - 1)(after_weights)
        have_resp(h, 1)
        vr = RB[h, 1].reshape(-1, D)
        VT[:, KEYS:] = vr.T
        probs = [weight * inv for weight in weights]
        halves = [prob.astype(BF16) for prob in probs]
        out = functools.reduce(
            jnp.add, [dot(VT[:, i * TILE : (i + 1) * TILE], half, NN) for i, half in enumerate(halves)]
        )
        out = (out * live_cols).astype(BF16).astype(F32)
        for j, col in enumerate(cols):
            o_ref[:, col] = out[:, j * RT : (j + 1) * RT].T.astype(BF16)
        row_dot = jnp.sum(gs.astype(F32).T * out, 0, keepdims=True)
        pl.when(h > 1)(lambda: step3(h - 2))

        def tile_grads(i, values):
            ds = (probs[i] * (dot(values, gs, NT) - row_dot)).astype(BF16)
            DS[h % SLOTS, i * TILE : (i + 1) * TILE] = ds
            return dot(ds, qs, NN), dot(halves[i], gs, NN)

        for i, tile in enumerate(tiles):
            grads = tile_grads(i, vp[tile])
            for t in (0, 1):
                AP[h, i // 2, t, i % 2 * 8 : i % 2 * 8 + 8] = grads[t].reshape(8, SIDE, 8, D)
        c0(h).start()
        pl.when(h > 0)(lambda: step2(h - 1))
        for i, tile in enumerate(tiles):
            for_keys, for_values = tile_grads(len(tiles) + i, vr[tile])
            T[h, i, :, 0] = (for_keys * SCALE).astype(BF16).reshape(2, RT, D)
            T[h, i, :, 1] = for_values.astype(BF16).reshape(2, RT, D)
        d0(h).start()
        return 0

    lax.fori_loop(0, HEADS, head, 0)
    dq_part(0)
    step1_prompt(3)
    step1_resp(3)
    dq_part(1)
    step3(2)
    dq_part(2)
    dq_part(3)
    step2(3)
    step3(3)

    for k in (1, 2, 3):
        a1(0, k).wait_send()
        a1(1, k).wait_send()

    def sent(h, _):
        a2_all(h).wait_send()
        a3(h).wait_send()
        c1_all(h).wait_send()
        c0(h).wait_send()
        d0(h).wait_send()
        b_sib(h, 0, 0).wait_send()
        b_sib(h, 1, 0).wait_send()
        for k in (1, 2, 3):
            c2(h, k).wait_send()

            def conditional(k=k):
                b_sib(h, 0, k).wait_send()
                b_sib(h, 1, k).wait_send()
                d1(h, k).wait_send()

            pl.when(zh - k >= 0)(conditional)

            def sent_on(k=k):
                b(h, 0, k).wait_send()
                b(h, 1, k).wait_send()

            pl.when(zh + k < SIDE)(sent_on)
        return 0

    lax.fori_loop(0, HEADS, sent, 0)


def hand_over(*refs):
    n = (len(refs) - 1) // 2
    copies = [pltpu.make_async_copy(refs[i], refs[n + i], refs[-1].at[i]) for i in range(n)]
    for copy in copies:
        copy.start()
    for copy in copies:
        copy.wait()


def body(queries, response_key_rows, response_value_rows, prompt_keys, prompt_value_rows, out_grad, lengths):
    dma = pltpu.SemaphoreType.DMA
    vmem = pl.BlockSpec(memory_space=pltpu.VMEM)
    hbm = pl.BlockSpec(memory_space=pl.ANY)
    scratch = [
        pltpu.VMEM((RT, HEADS * GROUP * D), BF16),
        pltpu.VMEM((RT, HEADS * GROUP * D), BF16),
        dma,
        dma,
        pltpu.VMEM((2, KEYS, D), BF16),
        pltpu.VMEM((HEADS, D, 2 * KEYS), BF16),
        pltpu.VMEM((D, 2 * KEYS), BF16),
        pltpu.VMEM((SLOTS, 2 * KEYS, GROUP * RT), BF16),
        pltpu.VMEM((8 * RT, RT), F32),
        pltpu.VMEM((2, HEADS, PLANE, SIDE, 16, D), BF16),
        pltpu.VMEM((HEADS, 2, 8, RT, D), BF16),
        pltpu.VMEM((HEADS, 2, 2, PLANE, SIDE, 8, D), F32),
        pltpu.VMEM((HEADS, SIDE, 2, 2, RT, D), BF16),
        pltpu.VMEM((HEADS, 2, PLANE, SIDE, 8, D), F32),
        pltpu.VMEM((HEADS, PLANE - 1, 2, SIDE, 8, D), F32),
        pltpu.VMEM((HEADS, 3, 2, 8, D), F32),
        pltpu.VMEM((HEADS, SIDE, 2, RT, D), BF16),
        pltpu.VMEM((HEADS, 3, 2, RT, D), BF16),
    ]
    per_peer = dma((HEADS, 3))
    per_head = dma((HEADS,))
    sems = [dma((2, 3))] * 2 + [per_head] * 4 + [dma((HEADS, 2, 3))] * 2 + [dma((HEADS, 2, 4))] * 2
    sems += [per_head] * 4 + [per_peer] * 2 + [per_head] * 2 + [per_peer] * 2
    wide = jax.ShapeDtypeStruct(queries.shape[1:], BF16)
    rows = jax.ShapeDtypeStruct(response_key_rows.shape[1:], BF16)
    shared = jax.ShapeDtypeStruct(prompt_keys.shape, F32)
    shapes = [wide, wide, rows, rows, shared, shared]
    results = pl.pallas_call(
        kernel,
        out_shape=shapes,
        in_specs=[hbm] * 2 + [vmem] * 4 + [pl.BlockSpec(memory_space=pltpu.SMEM)],
        out_specs=[vmem] * 6,
        scratch_shapes=scratch + sems,
        compiler_params=pltpu.CompilerParams(
            collective_id=0, has_side_effects=True, vmem_limit_bytes=60 * 2**20
        ),
        cost_estimate=pl.CostEstimate(flops=13 * 10**9, bytes_accessed=5 * 2**20, transcendentals=2**23),
    )(queries[0], out_grad[0], response_key_rows[0], response_value_rows[0], prompt_keys, prompt_value_rows, lengths)
    out, dq, drk, drv, dpk, dpv = pl.pallas_call(
        hand_over,
        out_shape=shapes,
        in_specs=[vmem] * 6,
        out_specs=[hbm] * 6,
        scratch_shapes=[dma((6,))],
    )(*results)
    return out[None], dq[None], drk[None], drv[None], dpk, dpv


def solution(mesh):
    rows = P(("grp", "resp"), "prompt", None)
    shared = P(("grp", "prompt", "resp"), None)
    return jax.shard_map(
        body,
        mesh=mesh,
        in_specs=(rows, rows, rows, shared, shared, rows, P("grp")),
        out_specs=(rows, rows, rows, rows, shared, shared),
        check_vma=False,
    )
```

```python
import functools

import jax
import jax.numpy as jnp
from jax import lax
from jax.experimental import pallas as pl
from jax.experimental.pallas import tpu as pltpu
from jax.sharding import PartitionSpec as P

F32 = jnp.float32
BF16 = jnp.bfloat16
MESH = pl.DeviceIdType.MESH

HEADS = 4
GROUP = 8
D = 128
RT = 128
SIDE = 4
PLANE = 16
SLOTS = 4
TILE = 256
KEYS = 1024
SCALE = D**-0.5
SCALE_LOG2E = SCALE * 1.4426950408889634

NT = (((1,), (1,)), ((), ()))
NN = (((1,), (0,)), ((), ()))
TN = (((0,), (0,)), ((), ()))


def dot(a, b, dims):
    return lax.dot_general(a, b, dims, preferred_element_type=F32)


def kernel(
    q_ref, g_ref, kr_ref, vr_ref, pk_ref, pv_ref, len_ref,
    o_ref, dq_ref, drk_ref, drv_ref, dpk_ref, dpv_ref,
    q_buf, g_buf, q_sem, g_sem, KV, KT, VT, DS, bias, G, RB, AP, T, c0r, c1r, c2r, d0r, d1r,
    a1_s, a1_r, a2_s, a2_r, a3_s, a3_r, b_s, b_r, bs_s, bs_r,
    c0_s, c0_r, c1_s, c1_r, c2_s, c2_r, d0_s, d0_r, d1_s, d1_r,
):
    p = lax.axis_index("prompt")
    r = lax.axis_index("resp")
    c = p % 2
    o = 1 - c
    zh = p // 2
    sib = {"prompt": zh * 2 + o}

    def z_peer(k):
        return {"prompt": ((zh + k) % SIDE) * 2 + c}

    def plane_peer(j):
        return {"resp": (r + j) % PLANE}

    def remote(src, dst, ss, rs, dev):
        return pltpu.make_async_remote_copy(
            src_ref=src, dst_ref=dst, send_sem=ss, recv_sem=rs, device_id=dev, device_id_type=MESH
        )

    peers = [sib] + [z_peer(k) for k in (1, 2, 3)] + [plane_peer(j) for j in range(1, PLANE)]
    barrier = pltpu.get_barrier_semaphore()
    for dev in peers:
        pl.semaphore_signal(barrier, inc=1, device_id=dev, device_id_type=MESH)
    mine = jnp.concatenate([pk_ref[...].astype(F32), pv_ref[...].astype(F32)], 0).astype(BF16)
    for h in range(HEADS):
        cols = slice(h * D, (h + 1) * D)
        RB[h, 0, p] = kr_ref[:, cols]
        RB[h, 1, p] = vr_ref[:, cols]
        G[c, h, r, zh] = mine[:, cols]
    pl.semaphore_wait(barrier, len(peers))

    def a1(part, k):
        block = G.at[c, 0:1, r, zh] if part == 0 else G.at[c, 1:HEADS, r, zh]
        return remote(block, block, a1_s.at[part, k - 1], a1_r.at[part, k - 1], z_peer(k))

    def a2_start(h):
        def send(j, _):
            remote(G.at[c, h, r], G.at[c, h, r], a2_s.at[h], a2_r.at[h], plane_peer(j)).start()
            return 0

        lax.fori_loop(1, PLANE, send, 0)

    def a2_all(h):
        rows = G.at[c, h, 0 : PLANE - 1]
        return remote(rows, rows, a2_s.at[h], a2_r.at[h], sib)

    def a3(h):
        return remote(G.at[c, h], G.at[c, h], a3_s.at[h], a3_r.at[h], sib)

    def b(h, t, k):
        return remote(RB.at[h, t, p], RB.at[h, t, p], b_s.at[h, t, k - 1], b_r.at[h, t, k - 1], z_peer(k))

    def b_sib(h, t, k):
        block = RB.at[h, t, ((zh - k + SIDE) % SIDE) * 2 + c]
        return remote(block, block, bs_s.at[h, t, k], bs_r.at[h, t, k], sib)

    def c0(h, t):
        return remote(AP.at[h, o, t], c0r.at[h, t], c0_s.at[h, t], c0_r.at[h, t], sib)

    def c1_start(h, t):
        def send(j, _):
            to = (r + j) % PLANE
            remote(AP.at[h, c, t, to], c1r.at[h, t, j - 1], c1_s.at[h, t], c1_r.at[h, t], {"resp": to}).start()
            return 0

        lax.fori_loop(1, PLANE, send, 0)

    def c1_all(h, t):
        return remote(c1r.at[h, t], c1r.at[h, t], c1_s.at[h, t], c1_r.at[h, t], sib)

    def c2(h, k):
        to = (zh + k) % SIDE
        return remote(AP.at[h, c, :, r, to], c2r.at[h, k - 1], c2_s.at[h, k - 1], c2_r.at[h, k - 1], z_peer(k))

    def d0(h, t):
        return remote(T.at[h, :, o, t], d0r.at[h, t], d0_s.at[h, t], d0_r.at[h, t], sib)

    def d1(h, t, k):
        to = (zh - k + SIDE) % SIDE
        return remote(
            T.at[h, to, c, t], d1r.at[h, k - 1, t], d1_s.at[h, t, k - 1], d1_r.at[h, t, k - 1], {"prompt": to * 2 + c}
        )

    def start_b(h):
        for t in (0, 1):
            b_sib(h, t, 0).start()
            for k in (1, 2, 3):
                pl.when(zh + k < SIDE)(lambda t=t, k=k: b(h, t, k).start())

    def relay_prompt(h):
        a2_all(h).wait_recv()
        a3(h).start()

    def relay_resp(h, t):
        for k in (1, 2, 3):

            def pass_on(k=k):
                b(h, t, k).wait_recv()
                b_sib(h, t, k).start()

            pl.when(zh - k >= 0)(pass_on)

    def have_resp(h, t):
        b_sib(h, t, 0).wait_recv()
        for k in (1, 2, 3):
            pl.when(zh - k >= 0)(lambda k=k: b_sib(h, t, k).wait_recv())

    def step1(h, t):
        c0(h, t).wait_recv()
        AP[h, c, t] += c0r[h, t]
        c1_start(h, t)
        d0(h, t).wait_recv()
        for k in (1, 2, 3):

            def pair(k=k):
                T[h, zh - k, c, t] = (T[h, zh - k, c, t].astype(F32) + d0r[h, t, zh - k].astype(F32)).astype(BF16)
                d1(h, t, k).start()

            pl.when(zh - k >= 0)(pair)

    def step2(h):
        c1_all(h, 0).wait_recv()
        c1_all(h, 1).wait_recv()
        total = AP[h, c, :, r]
        for j in range(PLANE - 1):
            total = total + c1r[h, :, j]
        AP[h, c, :, r] = total
        for k in (1, 2, 3):
            c2(h, k).start()

    def step3(h):
        for k in (1, 2, 3):

            def arrived(k=k):
                d1(h, 0, k).wait_recv()
                d1(h, 1, k).wait_recv()

            pl.when(zh + k < SIDE)(arrived)
        terms = T[h, zh, c].astype(F32) + d0r[h, :, zh].astype(F32)
        terms = terms + d1r[h, 0].astype(F32) + d1r[h, 1].astype(F32) + d1r[h, 2].astype(F32)
        cols = pl.ds(pl.multiple_of(h * D, D), D)
        drk_ref[:, cols] = terms[0].astype(BF16)
        drv_ref[:, cols] = terms[1].astype(BF16)
        for k in (1, 2, 3):
            c2(h, k).wait_recv()
        total = AP[h, c, :, r, zh] + c2r[h, 0] + c2r[h, 1] + c2r[h, 2]
        dpk_ref[:, cols] = total[0] * SCALE
        dpv_ref[:, cols] = total[1]

    for part in (0, 1):
        for k in (1, 2, 3):
            a1(part, k).start()
    start_b(0)
    q_in = pltpu.make_async_copy(q_ref, q_buf, q_sem)
    g_in = pltpu.make_async_copy(g_ref, g_buf, g_sem)
    q_in.start()
    g_in.start()
    for k in (1, 2, 3):
        a1(0, k).wait_recv()
    a2_start(0)
    for k in (1, 2, 3):

        def clear_b(k=k):
            RB[:, :, pl.ds((zh + k) * 2, 2)] = jnp.zeros((HEADS, 2, 2, RT, D), BF16)

        pl.when(zh + k < SIDE)(clear_b)

        def clear_d(k=k):
            d1r[:, k - 1] = jnp.zeros((HEADS, 2, RT, D), BF16)

        pl.when(zh + k >= SIDE)(clear_d)

    for k in (1, 2, 3):
        a1(1, k).wait_recv()
    for h in range(1, HEADS):
        a2_start(h)
    place = lax.broadcasted_iota(jnp.int32, (SIDE * 2 * RT, RT), 1) + p * RT
    key_place = lax.broadcasted_iota(jnp.int32, (SIDE * 2 * RT, RT), 0)
    bias[...] = jnp.where(key_place <= place, 0.0, -1e30).astype(F32)
    length = len_ref[r]
    live = (lax.broadcasted_iota(jnp.int32, (RT, 1), 0) + p * RT < length).astype(F32).astype(BF16)
    live = jnp.concatenate([live] * GROUP, 0)
    live_cols = (lax.broadcasted_iota(jnp.int32, (1, RT), 1) + p * RT < length).astype(F32)
    live_cols = jnp.concatenate([live_cols] * GROUP, 1)
    q_in.wait()
    g_in.wait()
    relay_prompt(0)
    relay_resp(0, 0)
    start_b(1)

    def dq_part(h):
        for_rows = dot(KT[h], DS[h % SLOTS], NN) * SCALE
        for j in range(GROUP):
            col = pl.ds(pl.multiple_of((h * GROUP + j) * D, D), D)
            dq_ref[:, col] = for_rows[:, j * RT : (j + 1) * RT].T.astype(BF16)

    def head(h, _):
        a3(h).wait_recv()
        for lane in (0, 1):
            rows = slice(lane * KEYS // 2, (lane + 1) * KEYS // 2)
            blocks = G[lane, h].astype(F32).reshape(PLANE * SIDE, 2, 8, D)
            KV[0, rows] = blocks[:, 0].reshape(-1, D).astype(BF16)
            KV[1, rows] = blocks[:, 1].reshape(-1, D).astype(BF16)
        kp, vp = KV[0], KV[1]
        KT[h, :, :KEYS] = kp.T
        VT[:, :KEYS] = vp.T
        cols = [pl.ds(pl.multiple_of((h * GROUP + j) * D, D), D) for j in range(GROUP)]
        qs = jnp.concatenate([q_buf[:, col] for col in cols], 0)
        gs = jnp.concatenate([g_buf[:, col] for col in cols], 0) * live

        tiles = [slice(first, first + TILE) for first in range(0, KEYS, TILE)]
        scores = [dot(kp[tile], qs, NT) for tile in tiles]
        top = functools.reduce(jnp.maximum, [jnp.max(score, 0, keepdims=True) for score in scores])
        have_resp(h, 0)
        kr = RB[h, 0].reshape(-1, D)
        KT[h, :, KEYS:] = kr.T
        for tile in tiles:
            score = dot(kr[tile], qs, NT) + jnp.concatenate([bias[tile]] * GROUP, 1)
            top = jnp.maximum(top, jnp.max(score, 0, keepdims=True))
            scores.append(score)
        pl.when(h > 0)(lambda: step1(h - 1, 0))
        pl.when(h == 0)(lambda: relay_resp(h, 1))
        pl.when(h < HEADS - 2)(lambda: start_b(h + 2))
        top = top * SCALE_LOG2E
        weights = [jnp.exp2(score * SCALE_LOG2E - top) for score in scores]
        inv = 1.0 / functools.reduce(jnp.add, [jnp.sum(weight, 0, keepdims=True) for weight in weights])

        def after_weights():
            relay_prompt(h + 1)
            relay_resp(h + 1, 0)
            relay_resp(h + 1, 1)

        pl.when(h < HEADS - 1)(after_weights)
        have_resp(h, 1)
        vr = RB[h, 1].reshape(-1, D)
        VT[:, KEYS:] = vr.T
        probs = [weight * inv for weight in weights]
        halves = [prob.astype(BF16) for prob in probs]
        for i in range(len(tiles)):
            for_values = dot(halves[i], gs, NN).reshape(8, SIDE, 8, D)
            AP[h, i // 2, 1, i % 2 * 8 : i % 2 * 8 + 8] = for_values
        c0(h, 1).start()
        for i in range(len(tiles)):
            for_values = dot(halves[len(tiles) + i], gs, NN)
            T[h, i, :, 1] = for_values.astype(BF16).reshape(2, RT, D)
        d0(h, 1).start()
        out = functools.reduce(
            jnp.add, [dot(VT[:, i * TILE : (i + 1) * TILE], half, NN) for i, half in enumerate(halves)]
        )
        out = (out * live_cols).astype(BF16).astype(F32)
        for j, col in enumerate(cols):
            o_ref[:, col] = out[:, j * RT : (j + 1) * RT].T.astype(BF16)
        row_dot = jnp.sum(gs.astype(F32).T * out, 0, keepdims=True)
        pl.when(h > 1)(lambda: step3(h - 2))

        def tile_grads(i, values):
            ds = (probs[i] * (dot(values, gs, NT) - row_dot)).astype(BF16)
            DS[h % SLOTS, i * TILE : (i + 1) * TILE] = ds
            return dot(ds, qs, NN)

        for i, tile in enumerate(tiles):
            AP[h, i // 2, 0, i % 2 * 8 : i % 2 * 8 + 8] = tile_grads(i, vp[tile]).reshape(8, SIDE, 8, D)
        c0(h, 0).start()
        step1(h, 1)
        pl.when(h > 0)(lambda: step2(h - 1))
        for i, tile in enumerate(tiles):
            T[h, i, :, 0] = (tile_grads(len(tiles) + i, vr[tile]) * SCALE).astype(BF16).reshape(2, RT, D)
        d0(h, 0).start()
        return 0

    lax.fori_loop(0, HEADS, head, 0)
    dq_part(0)
    step1(3, 0)
    dq_part(1)
    step3(2)
    dq_part(2)
    dq_part(3)
    step2(3)
    step3(3)

    for k in (1, 2, 3):
        a1(0, k).wait_send()
        a1(1, k).wait_send()

    def sent(h, _):
        a2_all(h).wait_send()
        a3(h).wait_send()
        for t in (0, 1):
            c0(h, t).wait_send()
            c1_all(h, t).wait_send()
            d0(h, t).wait_send()
        b_sib(h, 0, 0).wait_send()
        b_sib(h, 1, 0).wait_send()
        for k in (1, 2, 3):
            c2(h, k).wait_send()

            def conditional(k=k):
                b_sib(h, 0, k).wait_send()
                b_sib(h, 1, k).wait_send()
                d1(h, 0, k).wait_send()
                d1(h, 1, k).wait_send()

            pl.when(zh - k >= 0)(conditional)

            def sent_on(k=k):
                b(h, 0, k).wait_send()
                b(h, 1, k).wait_send()

            pl.when(zh + k < SIDE)(sent_on)
        return 0

    lax.fori_loop(0, HEADS, sent, 0)


def hand_over(*refs):
    n = (len(refs) - 1) // 2
    copies = [pltpu.make_async_copy(refs[i], refs[n + i], refs[-1].at[i]) for i in range(n)]
    for copy in copies:
        copy.start()
    for copy in copies:
        copy.wait()


def body(queries, response_key_rows, response_value_rows, prompt_keys, prompt_value_rows, out_grad, lengths):
    dma = pltpu.SemaphoreType.DMA
    vmem = pl.BlockSpec(memory_space=pltpu.VMEM)
    hbm = pl.BlockSpec(memory_space=pl.ANY)
    scratch = [
        pltpu.VMEM((RT, HEADS * GROUP * D), BF16),
        pltpu.VMEM((RT, HEADS * GROUP * D), BF16),
        dma,
        dma,
        pltpu.VMEM((2, KEYS, D), BF16),
        pltpu.VMEM((HEADS, D, 2 * KEYS), BF16),
        pltpu.VMEM((D, 2 * KEYS), BF16),
        pltpu.VMEM((SLOTS, 2 * KEYS, GROUP * RT), BF16),
        pltpu.VMEM((8 * RT, RT), F32),
        pltpu.VMEM((2, HEADS, PLANE, SIDE, 16, D), BF16),
        pltpu.VMEM((HEADS, 2, 8, RT, D), BF16),
        pltpu.VMEM((HEADS, 2, 2, PLANE, SIDE, 8, D), F32),
        pltpu.VMEM((HEADS, SIDE, 2, 2, RT, D), BF16),
        pltpu.VMEM((HEADS, 2, PLANE, SIDE, 8, D), F32),
        pltpu.VMEM((HEADS, 2, PLANE - 1, SIDE, 8, D), F32),
        pltpu.VMEM((HEADS, 3, 2, 8, D), F32),
        pltpu.VMEM((HEADS, 2, SIDE, RT, D), BF16),
        pltpu.VMEM((HEADS, 3, 2, RT, D), BF16),
    ]
    per_peer = dma((HEADS, 3))
    per_head = dma((HEADS,))
    sems = [dma((2, 3))] * 2 + [per_head] * 4 + [dma((HEADS, 2, 3))] * 2 + [dma((HEADS, 2, 4))] * 2
    per_type = dma((HEADS, 2))
    sems += [per_type] * 4 + [per_peer] * 2 + [per_type] * 2 + [dma((HEADS, 2, 3))] * 2
    wide = jax.ShapeDtypeStruct(queries.shape[1:], BF16)
    rows = jax.ShapeDtypeStruct(response_key_rows.shape[1:], BF16)
    shared = jax.ShapeDtypeStruct(prompt_keys.shape, F32)
    shapes = [wide, wide, rows, rows, shared, shared]
    results = pl.pallas_call(
        kernel,
        out_shape=shapes,
        in_specs=[hbm] * 2 + [vmem] * 4 + [pl.BlockSpec(memory_space=pltpu.SMEM)],
        out_specs=[vmem] * 6,
        scratch_shapes=scratch + sems,
        compiler_params=pltpu.CompilerParams(
            collective_id=0, has_side_effects=True, vmem_limit_bytes=60 * 2**20
        ),
        cost_estimate=pl.CostEstimate(flops=13 * 10**9, bytes_accessed=5 * 2**20, transcendentals=2**23),
    )(queries[0], out_grad[0], response_key_rows[0], response_value_rows[0], prompt_keys, prompt_value_rows, lengths)
    out, dq, drk, drv, dpk, dpv = pl.pallas_call(
        hand_over,
        out_shape=shapes,
        in_specs=[vmem] * 6,
        out_specs=[hbm] * 6,
        scratch_shapes=[dma((6,))],
    )(*results)
    return out[None], dq[None], drk[None], drv[None], dpk, dpv


def solution(mesh):
    rows = P(("grp", "resp"), "prompt", None)
    shared = P(("grp", "prompt", "resp"), None)
    return jax.shard_map(
        body,
        mesh=mesh,
        in_specs=(rows, rows, rows, shared, shared, rows, P("grp")),
        out_specs=(rows, rows, rows, rows, shared, shared),
        check_vma=False,
    )
```

```python
import functools

import jax
import jax.numpy as jnp
from jax import lax
from jax.experimental import pallas as pl
from jax.experimental.pallas import tpu as pltpu
from jax.sharding import PartitionSpec as P

F32 = jnp.float32
BF16 = jnp.bfloat16
MESH = pl.DeviceIdType.MESH

HEADS = 4
GROUP = 8
D = 128
RT = 128
SIDE = 4
PLANE = 16
SLOTS = 4
TILE = 256
KEYS = 1024
SCALE = D**-0.5
SCALE_LOG2E = SCALE * 1.4426950408889634

NT = (((1,), (1,)), ((), ()))
NN = (((1,), (0,)), ((), ()))
TN = (((0,), (0,)), ((), ()))


def dot(a, b, dims):
    return lax.dot_general(a, b, dims, preferred_element_type=F32)


def kernel(
    q_ref, g_ref, kr_ref, vr_ref, pk_ref, pv_ref, len_ref,
    o_ref, dq_ref, drk_ref, drv_ref, dpk_ref, dpv_ref,
    q_buf, g_buf, q_sem, g_sem, KV, KT, VT, DS, bias, G, RB, AP, T, c0r, c1r, c2r, d0r, d1r,
    a1_s, a1_r, a2_s, a2_r, a3_s, a3_r, b_s, b_r, bs_s, bs_r,
    c0_s, c0_r, c1_s, c1_r, c2_s, c2_r, d0_s, d0_r, d1_s, d1_r,
):
    p = lax.axis_index("prompt")
    r = lax.axis_index("resp")
    c = p % 2
    o = 1 - c
    zh = p // 2
    sib = {"prompt": zh * 2 + o}

    def z_peer(k):
        return {"prompt": ((zh + k) % SIDE) * 2 + c}

    def plane_peer(j):
        return {"resp": (r + j) % PLANE}

    def remote(src, dst, ss, rs, dev):
        return pltpu.make_async_remote_copy(
            src_ref=src, dst_ref=dst, send_sem=ss, recv_sem=rs, device_id=dev, device_id_type=MESH
        )

    peers = [sib] + [z_peer(k) for k in (1, 2, 3)] + [plane_peer(j) for j in range(1, PLANE)]
    barrier = pltpu.get_barrier_semaphore()
    for dev in peers:
        pl.semaphore_signal(barrier, inc=1, device_id=dev, device_id_type=MESH)
    mine = jnp.concatenate([pk_ref[...].astype(F32), pv_ref[...].astype(F32)], 0).astype(BF16)
    for h in range(HEADS):
        cols = slice(h * D, (h + 1) * D)
        RB[h, 0, p] = kr_ref[:, cols]
        RB[h, 1, p] = vr_ref[:, cols]
        G[c, h, r, zh] = mine[:, cols]
    pl.semaphore_wait(barrier, len(peers))

    def a1(part, k):
        block = G.at[c, 0:1, r, zh] if part == 0 else G.at[c, 1:HEADS, r, zh]
        return remote(block, block, a1_s.at[part, k - 1], a1_r.at[part, k - 1], z_peer(k))

    def a2_start(h):
        def send(j, _):
            remote(G.at[c, h, r], G.at[c, h, r], a2_s.at[h], a2_r.at[h], plane_peer(j)).start()
            return 0

        lax.fori_loop(1, PLANE, send, 0)

    def a2_all(h):
        rows = G.at[c, h, 0 : PLANE - 1]
        return remote(rows, rows, a2_s.at[h], a2_r.at[h], sib)

    def a3(h):
        return remote(G.at[c, h], G.at[c, h], a3_s.at[h], a3_r.at[h], sib)

    def b(h, t, k):
        return remote(RB.at[h, t, p], RB.at[h, t, p], b_s.at[h, t, k - 1], b_r.at[h, t, k - 1], z_peer(k))

    def b_sib(h, t, k):
        block = RB.at[h, t, ((zh - k + SIDE) % SIDE) * 2 + c]
        return remote(block, block, bs_s.at[h, t, k], bs_r.at[h, t, k], sib)

    def c0(h, t):
        return remote(AP.at[h, o, t], c0r.at[h, t], c0_s.at[h, t], c0_r.at[h, t], sib)

    def c1_start(h, t):
        def send(j, _):
            to = (r + j) % PLANE
            remote(AP.at[h, c, t, to], c1r.at[h, t, j - 1], c1_s.at[h, t], c1_r.at[h, t], {"resp": to}).start()
            return 0

        lax.fori_loop(1, PLANE, send, 0)

    def c1_all(h, t):
        return remote(c1r.at[h, t], c1r.at[h, t], c1_s.at[h, t], c1_r.at[h, t], sib)

    def c2(h, k):
        to = (zh + k) % SIDE
        return remote(AP.at[h, c, :, r, to], c2r.at[h, k - 1], c2_s.at[h, k - 1], c2_r.at[h, k - 1], z_peer(k))

    def d0(h, t):
        return remote(T.at[h, :, o, t], d0r.at[h, t], d0_s.at[h, t], d0_r.at[h, t], sib)

    def d1(h, t, k):
        to = (zh - k + SIDE) % SIDE
        return remote(
            T.at[h, to, c, t], d1r.at[h, k - 1, t], d1_s.at[h, t, k - 1], d1_r.at[h, t, k - 1], {"prompt": to * 2 + c}
        )

    def start_b(h):
        for t in (0, 1):
            b_sib(h, t, 0).start()
            for k in (1, 2, 3):
                pl.when(zh + k < SIDE)(lambda t=t, k=k: b(h, t, k).start())

    def relay_prompt(h):
        a2_all(h).wait_recv()
        a3(h).start()

    def relay_resp(h, t):
        for k in (1, 2, 3):

            def pass_on(k=k):
                b(h, t, k).wait_recv()
                b_sib(h, t, k).start()

            pl.when(zh - k >= 0)(pass_on)

    def have_resp(h, t):
        b_sib(h, t, 0).wait_recv()
        for k in (1, 2, 3):
            pl.when(zh - k >= 0)(lambda k=k: b_sib(h, t, k).wait_recv())

    def step1(h, t):
        step1_prompt(h, t)
        step1_resp(h, t)

    def step1_prompt(h, t):
        c0(h, t).wait_recv()
        AP[h, c, t] += c0r[h, t]
        c1_start(h, t)

    def step1_resp(h, t):
        d0(h, t).wait_recv()
        for k in (1, 2, 3):

            def pair(k=k):
                T[h, zh - k, c, t] = (T[h, zh - k, c, t].astype(F32) + d0r[h, t, zh - k].astype(F32)).astype(BF16)
                d1(h, t, k).start()

            pl.when(zh - k >= 0)(pair)

    def step2(h):
        c1_all(h, 0).wait_recv()
        c1_all(h, 1).wait_recv()
        total = AP[h, c, :, r]
        for j in range(PLANE - 1):
            total = total + c1r[h, :, j]
        AP[h, c, :, r] = total
        for k in (1, 2, 3):
            c2(h, k).start()

    def step3(h):
        for k in (1, 2, 3):

            def arrived(k=k):
                d1(h, 0, k).wait_recv()
                d1(h, 1, k).wait_recv()

            pl.when(zh + k < SIDE)(arrived)
        terms = T[h, zh, c].astype(F32) + d0r[h, :, zh].astype(F32)
        terms = terms + d1r[h, 0].astype(F32) + d1r[h, 1].astype(F32) + d1r[h, 2].astype(F32)
        cols = pl.ds(pl.multiple_of(h * D, D), D)
        drk_ref[:, cols] = terms[0].astype(BF16)
        drv_ref[:, cols] = terms[1].astype(BF16)
        for k in (1, 2, 3):
            c2(h, k).wait_recv()
        total = AP[h, c, :, r, zh] + c2r[h, 0] + c2r[h, 1] + c2r[h, 2]
        dpk_ref[:, cols] = total[0] * SCALE
        dpv_ref[:, cols] = total[1]

    for part in (0, 1):
        for k in (1, 2, 3):
            a1(part, k).start()
    start_b(0)
    q_in = pltpu.make_async_copy(q_ref, q_buf, q_sem)
    g_in = pltpu.make_async_copy(g_ref, g_buf, g_sem)
    q_in.start()
    g_in.start()
    for k in (1, 2, 3):
        a1(0, k).wait_recv()
    a2_start(0)
    for k in (1, 2, 3):

        def clear_b(k=k):
            RB[:, :, pl.ds((zh + k) * 2, 2)] = jnp.zeros((HEADS, 2, 2, RT, D), BF16)

        pl.when(zh + k < SIDE)(clear_b)

        def clear_d(k=k):
            d1r[:, k - 1] = jnp.zeros((HEADS, 2, RT, D), BF16)

        pl.when(zh + k >= SIDE)(clear_d)

    for k in (1, 2, 3):
        a1(1, k).wait_recv()
    for h in range(1, HEADS):
        a2_start(h)
    place = lax.broadcasted_iota(jnp.int32, (SIDE * 2 * RT, RT), 1) + p * RT
    key_place = lax.broadcasted_iota(jnp.int32, (SIDE * 2 * RT, RT), 0)
    bias[...] = jnp.where(key_place <= place, 0.0, -1e30).astype(F32)
    length = len_ref[r]
    live = (lax.broadcasted_iota(jnp.int32, (RT, 1), 0) + p * RT < length).astype(F32).astype(BF16)
    live = jnp.concatenate([live] * GROUP, 0)
    live_cols = (lax.broadcasted_iota(jnp.int32, (1, RT), 1) + p * RT < length).astype(F32)
    live_cols = jnp.concatenate([live_cols] * GROUP, 1)
    q_in.wait()
    g_in.wait()
    relay_prompt(0)
    relay_resp(0, 0)
    start_b(1)

    def dq_part(h):
        for_rows = dot(KT[h], DS[h % SLOTS], NN) * SCALE
        for j in range(GROUP):
            col = pl.ds(pl.multiple_of((h * GROUP + j) * D, D), D)
            dq_ref[:, col] = for_rows[:, j * RT : (j + 1) * RT].T.astype(BF16)

    def head(h, _):
        a3(h).wait_recv()
        for lane in (0, 1):
            rows = slice(lane * KEYS // 2, (lane + 1) * KEYS // 2)
            blocks = G[lane, h].astype(F32).reshape(PLANE * SIDE, 2, 8, D)
            KV[0, rows] = blocks[:, 0].reshape(-1, D).astype(BF16)
            KV[1, rows] = blocks[:, 1].reshape(-1, D).astype(BF16)
        kp, vp = KV[0], KV[1]
        KT[h, :, :KEYS] = kp.T
        VT[:, :KEYS] = vp.T
        cols = [pl.ds(pl.multiple_of((h * GROUP + j) * D, D), D) for j in range(GROUP)]
        qs = jnp.concatenate([q_buf[:, col] for col in cols], 0)
        gs = jnp.concatenate([g_buf[:, col] for col in cols], 0) * live

        tiles = [slice(first, first + TILE) for first in range(0, KEYS, TILE)]
        scores = [dot(kp[tile], qs, NT) for tile in tiles]
        top = functools.reduce(jnp.maximum, [jnp.max(score, 0, keepdims=True) for score in scores])
        have_resp(h, 0)
        kr = RB[h, 0].reshape(-1, D)
        KT[h, :, KEYS:] = kr.T
        for tile in tiles:
            score = dot(kr[tile], qs, NT) + jnp.concatenate([bias[tile]] * GROUP, 1)
            top = jnp.maximum(top, jnp.max(score, 0, keepdims=True))
            scores.append(score)
        pl.when(h > 0)(lambda: step1(h - 1, 0))
        pl.when(h == 0)(lambda: relay_resp(h, 1))
        pl.when(h < HEADS - 2)(lambda: start_b(h + 2))
        top = top * SCALE_LOG2E
        weights = [jnp.exp2(score * SCALE_LOG2E - top) for score in scores]
        inv = 1.0 / functools.reduce(jnp.add, [jnp.sum(weight, 0, keepdims=True) for weight in weights])

        def after_weights():
            relay_prompt(h + 1)
            relay_resp(h + 1, 0)
            relay_resp(h + 1, 1)

        pl.when(h < HEADS - 1)(after_weights)
        have_resp(h, 1)
        vr = RB[h, 1].reshape(-1, D)
        VT[:, KEYS:] = vr.T
        probs = [weight * inv for weight in weights]
        halves = [prob.astype(BF16) for prob in probs]
        for i in range(len(tiles)):
            for_values = dot(halves[i], gs, NN).reshape(8, SIDE, 8, D)
            AP[h, i // 2, 1, i % 2 * 8 : i % 2 * 8 + 8] = for_values
        c0(h, 1).start()
        for i in range(len(tiles)):
            for_values = dot(halves[len(tiles) + i], gs, NN)
            T[h, i, :, 1] = for_values.astype(BF16).reshape(2, RT, D)
        d0(h, 1).start()
        out = functools.reduce(
            jnp.add, [dot(VT[:, i * TILE : (i + 1) * TILE], half, NN) for i, half in enumerate(halves)]
        )
        out = (out * live_cols).astype(BF16).astype(F32)
        for j, col in enumerate(cols):
            o_ref[:, col] = out[:, j * RT : (j + 1) * RT].T.astype(BF16)
        row_dot = jnp.sum(gs.astype(F32).T * out, 0, keepdims=True)
        step1(h, 1)
        pl.when(h > 1)(lambda: step3(h - 2))

        def tile_grads(i, values):
            ds = (probs[i] * (dot(values, gs, NT) - row_dot)).astype(BF16)
            DS[h % SLOTS, i * TILE : (i + 1) * TILE] = ds
            return dot(ds, qs, NN)

        for i, tile in enumerate(tiles):
            AP[h, i // 2, 0, i % 2 * 8 : i % 2 * 8 + 8] = tile_grads(i, vp[tile]).reshape(8, SIDE, 8, D)
        c0(h, 0).start()
        pl.when(h > 0)(lambda: step2(h - 1))
        for i, tile in enumerate(tiles):
            T[h, i, :, 0] = (tile_grads(len(tiles) + i, vr[tile]) * SCALE).astype(BF16).reshape(2, RT, D)
        d0(h, 0).start()
        return 0

    lax.fori_loop(0, HEADS, head, 0)
    step1_prompt(3, 0)
    dq_part(0)
    step1_resp(3, 0)
    dq_part(1)
    step3(2)
    dq_part(2)
    dq_part(3)
    step2(3)
    step3(3)

    for k in (1, 2, 3):
        a1(0, k).wait_send()
        a1(1, k).wait_send()

    def sent(h, _):
        a2_all(h).wait_send()
        a3(h).wait_send()
        for t in (0, 1):
            c0(h, t).wait_send()
            c1_all(h, t).wait_send()
            d0(h, t).wait_send()
        b_sib(h, 0, 0).wait_send()
        b_sib(h, 1, 0).wait_send()
        for k in (1, 2, 3):
            c2(h, k).wait_send()

            def conditional(k=k):
                b_sib(h, 0, k).wait_send()
                b_sib(h, 1, k).wait_send()
                d1(h, 0, k).wait_send()
                d1(h, 1, k).wait_send()

            pl.when(zh - k >= 0)(conditional)

            def sent_on(k=k):
                b(h, 0, k).wait_send()
                b(h, 1, k).wait_send()

            pl.when(zh + k < SIDE)(sent_on)
        return 0

    lax.fori_loop(0, HEADS, sent, 0)


def hand_over(*refs):
    (sources, targets, buffers), (in_sems, out_sems) = (refs[i : i + 6] for i in (0, 6, 12)), refs[18:]
    pieces = []
    for i, source in enumerate(sources):
        rows = source.shape[0]
        step = 32 if source.shape[1] > HEADS * D else rows
        pieces += [(i, slice(first, first + step)) for first in range(0, rows, step)]
    arrive = [
        pltpu.make_async_copy(sources[i].at[rows], buffers[i].at[rows], in_sems.at[n])
        for n, (i, rows) in enumerate(pieces)
    ]
    leave = [
        pltpu.make_async_copy(buffers[i].at[rows], targets[i].at[rows], out_sems.at[n])
        for n, (i, rows) in enumerate(pieces)
    ]
    for copy in arrive:
        copy.start()
    for before, after in zip(arrive, leave):
        before.wait()
        after.start()
    for copy in leave:
        copy.wait()


def body(queries, response_key_rows, response_value_rows, prompt_keys, prompt_value_rows, out_grad, lengths):
    dma = pltpu.SemaphoreType.DMA
    vmem = pl.BlockSpec(memory_space=pltpu.VMEM)
    hbm = pl.BlockSpec(memory_space=pl.ANY)
    scratch = [
        pltpu.VMEM((RT, HEADS * GROUP * D), BF16),
        pltpu.VMEM((RT, HEADS * GROUP * D), BF16),
        dma,
        dma,
        pltpu.VMEM((2, KEYS, D), BF16),
        pltpu.VMEM((HEADS, D, 2 * KEYS), BF16),
        pltpu.VMEM((D, 2 * KEYS), BF16),
        pltpu.VMEM((SLOTS, 2 * KEYS, GROUP * RT), BF16),
        pltpu.VMEM((8 * RT, RT), F32),
        pltpu.VMEM((2, HEADS, PLANE, SIDE, 16, D), BF16),
        pltpu.VMEM((HEADS, 2, 8, RT, D), BF16),
        pltpu.VMEM((HEADS, 2, 2, PLANE, SIDE, 8, D), F32),
        pltpu.VMEM((HEADS, SIDE, 2, 2, RT, D), BF16),
        pltpu.VMEM((HEADS, 2, PLANE, SIDE, 8, D), F32),
        pltpu.VMEM((HEADS, 2, PLANE - 1, SIDE, 8, D), F32),
        pltpu.VMEM((HEADS, 3, 2, 8, D), F32),
        pltpu.VMEM((HEADS, 2, SIDE, RT, D), BF16),
        pltpu.VMEM((HEADS, 3, 2, RT, D), BF16),
    ]
    per_peer = dma((HEADS, 3))
    per_head = dma((HEADS,))
    sems = [dma((2, 3))] * 2 + [per_head] * 4 + [dma((HEADS, 2, 3))] * 2 + [dma((HEADS, 2, 4))] * 2
    per_type = dma((HEADS, 2))
    sems += [per_type] * 4 + [per_peer] * 2 + [per_type] * 2 + [dma((HEADS, 2, 3))] * 2
    wide = jax.ShapeDtypeStruct(queries.shape[1:], BF16)
    rows = jax.ShapeDtypeStruct(response_key_rows.shape[1:], BF16)
    shared = jax.ShapeDtypeStruct(prompt_keys.shape, F32)
    shapes = [wide, wide, rows, rows, shared, shared]
    results = pl.pallas_call(
        kernel,
        out_shape=shapes,
        in_specs=[hbm] * 2 + [vmem] * 4 + [pl.BlockSpec(memory_space=pltpu.SMEM)],
        out_specs=[vmem] * 6,
        scratch_shapes=scratch + sems,
        compiler_params=pltpu.CompilerParams(
            collective_id=0, has_side_effects=True, vmem_limit_bytes=60 * 2**20
        ),
        cost_estimate=pl.CostEstimate(flops=13 * 10**9, bytes_accessed=5 * 2**20, transcendentals=2**23),
    )(queries[0], out_grad[0], response_key_rows[0], response_value_rows[0], prompt_keys, prompt_value_rows, lengths)
    out, dq, drk, drv, dpk, dpv = pl.pallas_call(
        hand_over,
        out_shape=shapes,
        in_specs=[hbm] * 6,
        out_specs=[hbm] * 6,
        scratch_shapes=[pltpu.VMEM(shape.shape, shape.dtype) for shape in shapes] + [dma((12,)), dma((12,))],
    )(*results)
    return out[None], dq[None], drk[None], drv[None], dpk, dpv


def solution(mesh):
    rows = P(("grp", "resp"), "prompt", None)
    shared = P(("grp", "prompt", "resp"), None)
    return jax.shard_map(
        body,
        mesh=mesh,
        in_specs=(rows, rows, rows, shared, shared, rows, P("grp")),
        out_specs=(rows, rows, rows, rows, shared, shared),
        check_vma=False,
    )
```
